32 devices in a mesh: row: 4 (over z), group: 8 (over y, x, core).
Axes of the slice: x: 2, y: 2, z: 4, core: 2. Of those that a mesh axis runs over, the one named last changes fastest.
Arguments:
- states: bfloat16 [8192, 8192], P('row', 'group'), may hold values from -1 to 1, as said below
- targets: float32 [8192, 128], P('row'), may hold values from -6 to 6
- ridge: float32 [128], replicated, may hold values from 0.5 to 8
Outputs:
- weights: float32 [8192, 128], P(('group', 'row'))
- residual: float32 [8192, 128], P('row')
The draws below stay inside these ranges and needn't reach their ends.
Inputs may be any that keep to these rules, and one draw needn't show every extreme that they name: Final hidden states of the model, one row a token.
All inputs are finite; a program needn't handle non-finite values.
Results may differ from the reference program's by a relative error of at most 0.0026.
Values may be sent and summed in bfloat16 or wider, within the bound.
No kernel may reach another device: no remote copies, remote signals or barrier semaphores. Data moves between devices by JAX's collectives and lax.ppermute only.
A program may use at most 64 MiB of HBM per device.

```python
import math
import jax
import jax.numpy as jnp
from jax import lax

D = 8192
OUTS = 128
ITERS = 3
TOKENS = 8192


def draw_states(key, part):
    key = jax.random.fold_in(key, 11)
    first, second = jax.random.split(key, 2)
    base = jax.random.normal(first, (TOKENS, D), jnp.float32)
    columns = jnp.exp(jax.random.uniform(second, (D,), jnp.float32, math.log(0.3), math.log(3.0)))
    values = base * columns
    return jnp.clip(values / math.sqrt(D), -1.0, 1.0).astype(jnp.bfloat16)


def steps_of(stream_key, shape, cuts, least, largest):
    level, own = 1.0, jax.random.fold_in(stream_key, 6)
    for dim, shards_of in cuts:
        steps = jnp.exp(jax.random.uniform(jax.random.fold_in(own, dim), (shards_of,), jnp.float32, least / len(cuts), largest / len(cuts)))
        level = level * jnp.repeat(steps, shape[dim] // shards_of).reshape([-1 if axis == dim else 1 for axis in range(len(shape))])
    return level


def gaussian(own_key, dims, deviation, reach, pieces=(), dtype=jnp.bfloat16):
    values = deviation * jax.random.normal(own_key, dims, jnp.float32)
    if pieces:
        values = values * steps_of(own_key, dims, pieces, -0.22, 0.18)
    return jnp.clip(values, -reach, reach).astype(dtype)


def setup_inputs(seed: int = 0) -> dict:
    streams_of = jax.random.split(jax.random.key(seed), 4)
    states = draw_states(jax.random.fold_in(streams_of[3], 71), 0)
    targets = gaussian(streams_of[1], (TOKENS, OUTS), 1.0, 6.0, ((0, 4),), jnp.float32)
    ridge = jnp.clip(jnp.exp(jax.random.uniform(streams_of[2], (OUTS,), jnp.float32, math.log(0.5), math.log(8.0))), 0.5, 8.0)
    return {"states": states, "targets": targets, "ridge": ridge}


def transposed(states, resid_b):
    return lax.dot_general(states, resid_b, (((0,), (0,)), ((), ())), preferred_element_type=jnp.float32)


def reference(states, targets, ridge):
    weights = jnp.zeros((D, OUTS), jnp.float32)
    residual = targets
    grad = transposed(states, residual.astype(jnp.bfloat16))
    direction = grad
    gamma = jnp.sum(grad * grad, axis=0)
    for step in range(ITERS):
        image = jnp.dot(states, direction.astype(jnp.bfloat16), preferred_element_type=jnp.float32)
        delta = jnp.sum(image * image, axis=0) + ridge * jnp.sum(direction * direction, axis=0)
        alpha = gamma / delta
        weights = weights + alpha * direction
        residual = residual - alpha * image
        if step + 1 < ITERS:
            grad = transposed(states, residual.astype(jnp.bfloat16)) - ridge * weights
            gamma_new = jnp.sum(grad * grad, axis=0)
            direction = grad + (gamma_new / gamma) * direction
            gamma = gamma_new
    return weights, residual
```

```python
import functools

import jax
import jax.numpy as jnp
from jax import lax
from jax.experimental import pallas as pl
from jax.experimental.pallas import tpu as pltpu
from jax.sharding import PartitionSpec as P

ITERS = 3
PAD = 16
F32 = jnp.float32
BF16 = jnp.bfloat16
ROW_WIRE = (F32, F32, F32)
CORE_WIRE = (F32, F32, F32)
CHIP_WIRE = (F32, F32, F32)
LIMIT = 24 * 1024 * 1024


def tree_sum(terms):
    terms = list(terms)
    while len(terms) > 1:
        terms = [terms[i] + terms[i + 1] for i in range(0, len(terms), 2)]
    return terms[0]


def put_row(ref, value):
    rows = ref.shape[0] - PAD
    if ref.dtype == F32:
        parts = [value]
    else:
        high = value.astype(BF16).astype(F32)
        middle = (value - high).astype(BF16).astype(F32)
        parts = [high, middle, value - high - middle]
    shape = (PAD, ref.shape[1])
    index = lax.broadcasted_iota(jnp.int32, shape, 0)
    block = jnp.zeros(shape, F32)
    for place, part in enumerate(parts):
        block = jnp.where(index == place, jnp.broadcast_to(part, shape), block)
    ref[pl.ds(rows, PAD), :] = block.astype(ref.dtype)


def get_row(ref):
    rows = ref.shape[0] - PAD
    return jnp.sum(ref[pl.ds(rows, PAD), :].astype(F32), axis=0, keepdims=True)


def body_of(ref):
    return ref[pl.ds(0, ref.shape[0] - PAD), :]


def column_sum(values):
    return jnp.sum(values, axis=0, keepdims=True)


def spread(ref, value):
    ref[...] = jnp.broadcast_to(value, ref.shape)


def call(kernel, outs, *operands):
    vmem = pl.BlockSpec(memory_space=pltpu.VMEM)
    return pl.pallas_call(
        kernel,
        out_shape=[jax.ShapeDtypeStruct(shape, dtype) for shape, dtype in outs],
        in_specs=[vmem] * len(operands),
        out_specs=[vmem] * len(outs),
        compiler_params=pltpu.CompilerParams(vmem_limit_bytes=LIMIT),
    )(*operands)


def call_scratch(kernel, outs, scratch, *operands):
    vmem = pl.BlockSpec(memory_space=pltpu.VMEM)
    return pl.pallas_call(
        kernel,
        out_shape=[jax.ShapeDtypeStruct(shape, dtype) for shape, dtype in outs],
        in_specs=[vmem] * len(operands),
        out_specs=[vmem] * len(outs),
        scratch_shapes=scratch,
        compiler_params=pltpu.CompilerParams(vmem_limit_bytes=LIMIT),
    )(*operands)


def shards(states, targets, ridge):
    n_row = lax.axis_size("row")
    n_group = lax.axis_size("group")
    n_chip = n_group // 2
    tokens, feats = states.shape
    outs = targets.shape[1]
    feat_share = feats // n_row
    tok_share = tokens // n_group
    half = tokens // 2
    ridge = ridge.reshape(1, outs)
    scalar = ((8, outs), F32)

    def over_row(step, value):
        return lax.ppermute(value, "row", [(i, i ^ step) for i in range(n_row)])

    def over_group(step, value):
        return lax.ppermute(value, "group", [(i, i ^ step) for i in range(n_group)])

    def row_place(step):
        return pl.multiple_of((lax.axis_index("row") ^ step) * feat_share, feat_share)

    def token_place(core_step, chip_step):
        me = lax.axis_index("group")
        core = (me % 2) ^ core_step
        chip = (me // 2) ^ chip_step
        return pl.multiple_of((core * n_chip + chip) * tok_share, tok_share)

    def backward(wire, from_targets, *blocks):
        def kernel(a_ref, *refs):
            ins = refs[: len(blocks)]
            own_ref, delta_ref, *msg_refs, vec, prod = refs[len(blocks) :]
            if from_targets:
                vec[...] = ins[0][...].astype(BF16)
                delta = jnp.zeros((1, outs), F32)
            else:
                for core_step in range(2):
                    for chip_step in range(n_chip):
                        ref = ins[core_step * n_chip + chip_step]
                        vec[pl.ds(token_place(core_step, chip_step), tok_share), :] = body_of(ref)
                delta = tree_sum([get_row(ref) for ref in ins])
            spread(delta_ref, delta)
            turned = vec[...].T
            for start in range(0, feats, 256):
                part = jnp.dot(turned, a_ref[:, start : start + 256], preferred_element_type=F32)
                prod[start : start + 256, :] = part.T
            own_ref[...] = prod[pl.ds(row_place(0), feat_share), :]
            for step, ref in enumerate(msg_refs, 1):
                ref[pl.ds(0, feat_share), :] = prod[pl.ds(row_place(step), feat_share), :].astype(wire)
                put_row(ref, delta)

        msgs = [((feat_share + PAD, outs), wire)] * (n_row - 1)
        result = call_scratch(
            kernel,
            [((feat_share, outs), F32), scalar] + msgs,
            [pltpu.VMEM((tokens, outs), BF16), pltpu.VMEM((feats, outs), F32)],
            states,
            *blocks,
        )
        own, delta, *sends = result
        got = [over_row(step, send) for step, send in enumerate(sends, 1)]
        return own, delta, got

    def begin(own, got):
        def kernel(own_ref, *refs):
            ins, (grad_ref, msg_ref) = refs[: n_row - 1], refs[n_row - 1 :]
            grad = own_ref[...]
            for ref in ins:
                grad = grad + body_of(ref).astype(F32)
            grad_ref[...] = grad
            msg_ref[pl.ds(0, feat_share), :] = grad.astype(BF16)
            put_row(msg_ref, column_sum(grad * grad))

        return call(
            kernel, [((feat_share, outs), F32), ((feat_share + PAD, outs), BF16)], own, *got
        )

    def advance(own, delta, got, gamma, grad, direction, image, weights, residual):
        def kernel(own_ref, delta_ref, *refs):
            ins = refs[: n_row - 1]
            gamma_ref, grad_ref, dir_ref, image_ref, w_ref, r_ref, ridge_ref = refs[n_row - 1 : n_row + 6]
            w_out, r_out, grad_out, msg_ref = refs[n_row + 6 :]
            delta_all = tree_sum([delta_ref[0:1, :]] + [get_row(ref) for ref in ins])
            alpha = gamma_ref[0:1, :] / delta_all
            prod = own_ref[...]
            for ref in ins:
                prod = prod + body_of(ref).astype(F32)
            w_out[...] = w_ref[...] + alpha * dir_ref[...]
            r_out[...] = r_ref[...] - alpha * image_ref[...]
            new = grad_ref[...] - alpha * (prod + ridge_ref[...] * dir_ref[...])
            grad_out[...] = new
            msg_ref[pl.ds(0, feat_share), :] = new.astype(BF16)
            put_row(msg_ref, column_sum(new * new))

        return call(
            kernel,
            [((feat_share, outs), F32), ((tok_share, outs), F32), ((feat_share, outs), F32),
             ((feat_share + PAD, outs), BF16)],
            own, delta, *got, gamma, grad, direction, image, weights, residual, ridge,
        )

    def forward(wire, msg):
        blocks = [msg] + [over_row(step, msg) for step in range(1, n_row)]

        def kernel(a_ref, *refs):
            ins = refs[:n_row]
            own_ref, gamma_ref, peer_ref, vec = refs[n_row:]
            for step, ref in enumerate(ins):
                vec[pl.ds(row_place(step), feat_share), :] = body_of(ref)
            gamma = tree_sum([get_row(ref) for ref in ins])
            spread(gamma_ref, gamma)
            for core_step, ref in ((1, peer_ref), (0, own_ref)):
                for chip_step in range(n_chip):
                    part = jnp.dot(
                        a_ref[pl.ds(token_place(core_step, chip_step), tok_share), :],
                        vec[...],
                        preferred_element_type=F32,
                    )
                    ref[pl.ds(chip_step * tok_share, tok_share), :] = part.astype(ref.dtype)
            put_row(peer_ref, gamma)

        own, gamma, peer = call_scratch(
            kernel,
            [((half, outs), F32), scalar, ((half + PAD, outs), wire)],
            [pltpu.VMEM((feats, outs), BF16)],
            states,
            *blocks,
        )
        return own, gamma, over_group(1, peer)

    def join_cores(wire, own, gamma, got):
        def kernel(own_ref, gamma_ref, got_ref, out_ref, gamma_out, *msg_refs):
            total = gamma_ref[0:1, :] + get_row(got_ref)
            spread(gamma_out, total)
            for step, ref in enumerate((out_ref,) + msg_refs):
                place = pl.ds(step * tok_share, tok_share)
                both = own_ref[place, :] + got_ref[place, :].astype(F32)
                ref[pl.ds(0, tok_share), :] = both.astype(ref.dtype)
                if step:
                    put_row(ref, total)

        msgs = [((tok_share + PAD, outs), wire)] * (n_chip - 1)
        own, gamma, *sends = call(
            kernel, [((tok_share, outs), F32), scalar] + msgs, own, gamma, got
        )
        return own, gamma, [over_group(2 * step, send) for step, send in enumerate(sends, 1)]

    def image_of(wire, own, gamma, got, grad, before):
        def kernel(own_ref, gamma_ref, *refs):
            ins = refs[: n_chip - 1]
            grad_ref, ridge_ref, *rest = refs[n_chip - 1 :]
            gamma_out, dir_out, image_out, msg_ref = rest[-4:]
            gamma_all = tree_sum([gamma_ref[0:1, :]] + [get_row(ref) for ref in ins])
            spread(gamma_out, gamma_all)
            image = own_ref[...]
            for ref in ins:
                image = image + body_of(ref).astype(F32)
            direction = grad_ref[...]
            if before:
                old_gamma, old_dir, old_image = rest[:3]
                beta = gamma_all / old_gamma[0:1, :]
                image = image + beta * old_image[...]
                direction = direction + beta * old_dir[...]
            image_out[...] = image
            dir_out[...] = direction
            msg_ref[pl.ds(0, tok_share), :] = image.astype(msg_ref.dtype)
            put_row(
                msg_ref,
                column_sum(image * image) + ridge_ref[...] * column_sum(direction * direction),
            )

        return call(
            kernel,
            [scalar, ((feat_share, outs), F32), ((tok_share, outs), F32),
             ((tok_share + PAD, outs), wire)],
            own, gamma, *got, grad, ridge, *before,
        )

    def gathered(msg):
        mine = [msg] + [over_group(2 * step, msg) for step in range(1, n_chip)]
        return mine + [over_group(1, block) for block in mine]

    def own_targets():
        me = lax.axis_index("group")
        place = ((me % 2) * n_chip + me // 2) * tok_share
        return lax.dynamic_slice_in_dim(targets, place, tok_share, 0)

    weights = jnp.zeros((feat_share, outs), F32)
    residual = own_targets()
    own, _, got = backward(ROW_WIRE[0], True, targets)
    grad, msg = begin(own, got)
    before = ()
    for step in range(ITERS):
        own, gamma, got = forward(CORE_WIRE[step], msg)
        own, gamma, got = join_cores(CHIP_WIRE[step], own, gamma, got)
        last = step + 1 == ITERS
        gamma, direction, image, msg = image_of(
            F32 if last else BF16, own, gamma, got, grad, before
        )
        blocks = gathered(msg)
        if not last:
            own, delta, got = backward(ROW_WIRE[step + 1], False, *blocks)
            weights, residual, grad, msg = advance(
                own, delta, got, gamma, grad, direction, image, weights, residual
            )
            before = (gamma, direction, image)

    def last_delta(*refs):
        *ins, out_ref = refs
        spread(out_ref, tree_sum([get_row(ref) for ref in ins]))

    (delta,) = call(last_delta, [scalar], *blocks)
    deltas = [delta] + [over_row(step, delta) for step in range(1, n_row)]
    kept = gathered(residual)

    def finish(*refs):
        delta_refs, refs = refs[:n_row], refs[n_row:]
        image_refs, refs = refs[:n_group], refs[n_group:]
        kept_refs, refs = refs[:n_group], refs[n_group:]
        gamma_ref, dir_ref, w_ref, w_out, r_out = refs
        alpha = gamma_ref[0:1, :] / tree_sum([ref[0:1, :] for ref in delta_refs])
        w_out[...] = w_ref[...] + alpha * dir_ref[...]
        for core_step in range(2):
            for chip_step in range(n_chip):
                index = core_step * n_chip + chip_step
                place = pl.ds(token_place(core_step, chip_step), tok_share)
                r_out[place, :] = kept_refs[index][...] - alpha * body_of(image_refs[index]).astype(F32)

    weights, residual = call(
        finish,
        [((feat_share, outs), F32), ((tokens, outs), F32)],
        *deltas, *blocks, *kept, gamma, direction, weights,
    )
    return weights, residual


def solution(mesh):
    placed = (P("row", "group"), P("row", None), P())
    return jax.shard_map(
        shards,
        mesh=mesh,
        in_specs=placed,
        out_specs=(P(("group", "row"), None), P("row", None)),
        check_vma=False,
    )
```

```python
import jax
import jax.numpy as jnp
from jax import lax
from jax.experimental import pallas as pl
from jax.experimental.pallas import tpu as pltpu
from jax.sharding import PartitionSpec as P

ITERS = 3
PAD = 16
F32 = jnp.float32
BF16 = jnp.bfloat16
ROW_WIRE = (F32, F32, BF16)
CORE_WIRE = (F32, F32, F32)
CHIP_WIRE = ((BF16, BF16), (BF16, BF16), (BF16, BF16))
LIMIT = 24 * 1024 * 1024


def tree_sum(terms):
    terms = list(terms)
    while len(terms) > 1:
        terms = [terms[i] + terms[i + 1] for i in range(0, len(terms), 2)]
    return terms[0]


def put_rows(ref, *values):
    rows = ref.shape[0] - PAD
    parts = []
    for value in values:
        high = value.astype(BF16).astype(F32)
        middle = (value - high).astype(BF16).astype(F32)
        parts += [high, middle, value - high - middle]
    shape = (PAD, ref.shape[1])
    index = lax.broadcasted_iota(jnp.int32, shape, 0)
    block = jnp.zeros(shape, F32)
    for place, part in enumerate(parts):
        block = jnp.where(index == place, jnp.broadcast_to(part, shape), block)
    ref[pl.ds(rows, PAD), :] = block.astype(ref.dtype)


def get_row(ref, which=0):
    rows = ref.shape[0] - PAD
    tail = ref[pl.ds(rows, PAD), :].astype(F32)
    at = 3 * which
    return tail[at : at + 1] + tail[at + 1 : at + 2] + tail[at + 2 : at + 3]


def body_of(ref):
    return ref[pl.ds(0, ref.shape[0] - PAD), :]


def column_sum(values):
    return jnp.sum(values, axis=0, keepdims=True)


def spread(ref, value):
    ref[...] = jnp.broadcast_to(value, ref.shape)


def call(kernel, outs, operands, scratch=()):
    vmem = pl.BlockSpec(memory_space=pltpu.VMEM)
    return pl.pallas_call(
        kernel,
        out_shape=[jax.ShapeDtypeStruct(shape, dtype) for shape, dtype in outs],
        in_specs=[vmem] * len(operands),
        out_specs=[vmem] * len(outs),
        scratch_shapes=scratch,
        compiler_params=pltpu.CompilerParams(vmem_limit_bytes=LIMIT),
    )(*operands)


def shards(states, targets, ridge):
    n_row = lax.axis_size("row")
    n_group = lax.axis_size("group")
    levels = (n_group // 2).bit_length() - 1
    tokens, feats = states.shape
    outs = targets.shape[1]
    feat_share = feats // n_row
    half = tokens // 2
    piece = half // levels
    block = 256
    ridge = ridge.reshape(1, outs)
    scalar = ((8, outs), F32)
    feature_rows = ((feat_share, outs), F32)
    token_rows = ((half, outs), F32)

    def over_row(step, value):
        return lax.ppermute(value, "row", [(i, i ^ step) for i in range(n_row)])

    def over_group(step, value):
        return lax.ppermute(value, "group", [(i, i ^ step) for i in range(n_group)])

    def row_place(step):
        return pl.multiple_of((lax.axis_index("row") ^ step) * feat_share, feat_share)

    def token_place(core_step):
        core = (lax.axis_index("group") % 2) ^ core_step
        return pl.multiple_of(core * half, half)

    def backward(wire, *blocks):
        first = len(blocks) == 1
        wide = 2 * outs if first else outs

        def kernel(a_ref, *refs):
            ins = refs[: len(blocks)]
            own_ref, delta_ref, *msg_refs, vec, prod = refs[len(blocks) :]
            if first:
                whole = ins[0][...]
                high = whole.astype(BF16)
                vec[:, 0:outs] = high
                vec[:, outs:wide] = (whole - high.astype(F32)).astype(BF16)
                delta = jnp.zeros((1, outs), F32)
            else:
                for core_step, ref in enumerate(ins):
                    vec[pl.ds(token_place(core_step), half), :] = body_of(ref)
                delta = get_row(ins[0]) + get_row(ins[1])
            spread(delta_ref, delta)
            turned = vec[...].T
            for start in range(0, feats, block):
                part = jnp.dot(turned, a_ref[:, start : start + block], preferred_element_type=F32)
                if first:
                    part = part[0:outs] + part[outs:wide]
                prod[start : start + block, :] = part.T
            own_ref[...] = prod[pl.ds(row_place(0), feat_share), :]
            for step, ref in enumerate(msg_refs, 1):
                ref[pl.ds(0, feat_share), :] = prod[pl.ds(row_place(step), feat_share), :].astype(wire)
                put_rows(ref, delta)

        msgs = [((feat_share + PAD, outs), wire)] * (n_row - 1)
        own, delta, *sends = call(
            kernel,
            [feature_rows, scalar] + msgs,
            (states,) + blocks,
            [pltpu.VMEM((tokens, wide), BF16), pltpu.VMEM((feats, outs), F32)],
        )
        return own, delta, [over_row(step, send) for step, send in enumerate(sends, 1)]

    def begin(own, got):
        def kernel(own_ref, *refs):
            ins, (grad_ref, msg_ref) = refs[: n_row - 1], refs[n_row - 1 :]
            grad = own_ref[...]
            for ref in ins:
                grad = grad + body_of(ref).astype(F32)
            grad_ref[...] = grad
            msg_ref[pl.ds(0, feat_share), :] = grad.astype(BF16)
            put_rows(msg_ref, column_sum(grad * grad), jnp.zeros((1, outs), F32))

        return call(kernel, [feature_rows, ((feat_share + PAD, outs), BF16)], [own] + got)

    def advance(own, delta, got, gamma, dir_sq, grad, direction, image, weights, residual):
        def kernel(own_ref, delta_ref, *refs):
            ins = refs[: n_row - 1]
            gamma_ref, sq_ref, grad_ref, dir_ref, image_ref, w_ref, r_ref, ridge_ref = refs[n_row - 1 : n_row + 7]
            w_out, r_out, grad_out, msg_ref = refs[n_row + 7 :]
            image_sq = tree_sum([delta_ref[0:1, :]] + [get_row(ref) for ref in ins])
            alpha = gamma_ref[0:1, :] / (image_sq + ridge_ref[...] * sq_ref[0:1, :])
            prod = own_ref[...]
            for ref in ins:
                prod = prod + body_of(ref).astype(F32)
            old_dir = dir_ref[...]
            new = grad_ref[...] - alpha * (prod + ridge_ref[...] * old_dir)
            msg_ref[pl.ds(0, feat_share), :] = new.astype(BF16)
            put_rows(msg_ref, column_sum(new * new), column_sum(new * old_dir))
            grad_out[...] = new
            w_out[...] = w_ref[...] + alpha * old_dir
            r_out[...] = r_ref[...] - alpha * image_ref[...]

        return call(
            kernel,
            [feature_rows, token_rows, feature_rows, ((feat_share + PAD, outs), BF16)],
            [own, delta, *got, gamma, dir_sq, grad, direction, image, weights, residual, ridge],
        )

    def forward(wire, msg):
        blocks = [msg] + [over_row(step, msg) for step in range(1, n_row)]

        def kernel(a_ref, *refs):
            ins = refs[:n_row]
            own_ref, gamma_ref, cross_ref, peer_ref, vec = refs[n_row:]
            for step, ref in enumerate(ins):
                vec[pl.ds(row_place(step), feat_share), :] = body_of(ref)
            gamma = tree_sum([get_row(ref, 0) for ref in ins])
            cross = tree_sum([get_row(ref, 1) for ref in ins])
            spread(gamma_ref, gamma)
            spread(cross_ref, cross)
            for core_step, ref in ((1, peer_ref), (0, own_ref)):
                for start in range(0, half, block):
                    part = jnp.dot(
                        a_ref[pl.ds(pl.multiple_of(token_place(core_step) + start, block), block), :],
                        vec[...],
                        preferred_element_type=F32,
                    )
                    ref[start : start + block, :] = part.astype(ref.dtype)
            put_rows(peer_ref, gamma, cross)

        own, gamma, cross, peer = call(
            kernel,
            [token_rows, scalar, scalar, ((half + PAD, outs), wire)],
            [states] + blocks,
            [pltpu.VMEM((feats, outs), BF16)],
        )
        return own, gamma, cross, over_group(1, peer)

    def pieces(wire):
        return [((piece + (0 if index else PAD), outs), wire) for index in range(levels)]

    def swapped(step, sends):
        return [
            over_group(2 << ((index + step) % levels), send) for index, send in enumerate(sends)
        ]

    def join_cores(wire, own, gamma, cross, got):
        def kernel(own_ref, gamma_ref, cross_ref, got_ref, *msg_refs):
            for index, ref in enumerate(msg_refs):
                place = pl.ds(index * piece, piece)
                both = own_ref[place, :] + got_ref[place, :].astype(F32)
                ref[pl.ds(0, piece), :] = both.astype(wire)
            put_rows(
                msg_refs[0],
                gamma_ref[0:1, :] + get_row(got_ref, 0),
                cross_ref[0:1, :] + get_row(got_ref, 1),
            )

        return call(kernel, pieces(wire), [own, gamma, cross, got])

    def join_chips(wire, sent, got):
        def kernel(*refs):
            mine, theirs, out_refs = refs[:levels], refs[levels : 2 * levels], refs[2 * levels :]
            for ref, own_ref, got_ref in zip(out_refs, mine, theirs):
                place = pl.ds(0, piece)
                both = own_ref[place, :].astype(F32) + got_ref[place, :].astype(F32)
                ref[place, :] = both.astype(wire)
            put_rows(out_refs[0], *[get_row(mine[0], k) + get_row(theirs[0], k) for k in range(2)])

        return call(kernel, pieces(wire), list(sent) + got)

    def image_of(wire, sent, got, grad, before):
        def kernel(*refs):
            mine, theirs = refs[:levels], refs[levels : 2 * levels]
            grad_ref, *rest = refs[2 * levels :]
            gamma_out, sq_out, dir_out, image_out, msg_ref, part_out = rest[-6:]
            gamma, cross = [get_row(mine[0], k) + get_row(theirs[0], k) for k in range(2)]
            spread(gamma_out, gamma)
            direction = grad_ref[...]
            dir_sq = gamma
            if before:
                old_gamma, old_sq, old_dir, old_image = rest[:4]
                beta = gamma / old_gamma[0:1, :]
                direction = direction + beta * old_dir[...]
                dir_sq = gamma + beta * (2.0 * cross + beta * old_sq[0:1, :])
            dir_out[...] = direction
            spread(sq_out, dir_sq)
            image_sq = jnp.zeros((1, outs), F32)
            for index, (own_ref, got_ref) in enumerate(zip(mine, theirs)):
                place = pl.ds(index * piece, piece)
                image = own_ref[pl.ds(0, piece), :].astype(F32) + got_ref[pl.ds(0, piece), :].astype(F32)
                if before:
                    image = image + beta * old_image[place, :]
                image_out[place, :] = image
                msg_ref[place, :] = image.astype(wire)
                image_sq = image_sq + column_sum(image * image)
            put_rows(msg_ref, image_sq)
            spread(part_out, image_sq)

        return call(
            kernel,
            [scalar, scalar, feature_rows, token_rows, ((half + PAD, outs), wire), scalar],
            list(sent) + got + [grad, *before],
        )

    core = lax.axis_index("group") % 2
    weights = jnp.zeros((feat_share, outs), F32)
    residual = lax.dynamic_slice_in_dim(targets, core * half, half, 0)
    own, _, got = backward(ROW_WIRE[0], targets)
    grad, msg = begin(own, got)
    before = ()
    for step in range(ITERS):
        own, gamma, cross, got = forward(CORE_WIRE[step], msg)
        sent = join_cores(CHIP_WIRE[step][0], own, gamma, cross, got)
        got = swapped(0, sent)
        for level in range(1, levels):
            sent = join_chips(CHIP_WIRE[step][1], sent, got)
            got = swapped(level, sent)
        last = step + 1 == ITERS
        gamma, dir_sq, direction, image, msg, part = image_of(
            F32 if last else BF16, sent, got, grad, before
        )
        if not last:
            own, delta, got = backward(ROW_WIRE[step + 1], msg, over_group(1, msg))
            weights, residual, grad, msg = advance(
                own, delta, got, gamma, dir_sq, grad, direction, image, weights, residual
            )
            before = (gamma, dir_sq, direction, image)

    def both_cores(own_ref, got_ref, out_ref):
        out_ref[...] = own_ref[...] + got_ref[...]

    (delta,) = call(both_cores, [scalar], [part, over_group(1, part)])
    other_image = over_group(1, image)
    other_residual = over_group(1, residual)
    deltas = [delta] + [over_row(step, delta) for step in range(1, n_row)]

    def finish(*refs):
        delta_refs, refs = refs[:n_row], refs[n_row:]
        gamma_ref, sq_ref, ridge_ref, image_ref, other_image_ref, r_ref, other_r_ref, dir_ref, w_ref, w_out, r_out = refs
        image_sq = tree_sum([ref[0:1, :] for ref in delta_refs])
        alpha = gamma_ref[0:1, :] / (image_sq + ridge_ref[...] * sq_ref[0:1, :])
        w_out[...] = w_ref[...] + alpha * dir_ref[...]
        r_out[pl.ds(token_place(0), half), :] = r_ref[...] - alpha * image_ref[...]
        r_out[pl.ds(token_place(1), half), :] = other_r_ref[...] - alpha * other_image_ref[...]

    weights, residual = call(
        finish,
        [feature_rows, ((tokens, outs), F32)],
        [*deltas, gamma, dir_sq, ridge, image, other_image, residual, other_residual, direction, weights],
    )
    return weights, residual


def solution(mesh):
    placed = (P("row", "group"), P("row", None), P())
    return jax.shard_map(
        shards,
        mesh=mesh,
        in_specs=placed,
        out_specs=(P(("group", "row"), None), P("row", None)),
        check_vma=False,
    )
```

```python
import jax
import jax.numpy as jnp
from jax import lax
from jax.experimental import pallas as pl
from jax.experimental.pallas import tpu as pltpu
from jax.sharding import PartitionSpec as P

ITERS = 3
PAD = 16
F32 = jnp.float32
BF16 = jnp.bfloat16
F16 = jnp.float16
ROW_WIRE = (F16, F16, BF16)
CORE_WIRE = (F32, F32, F32)
CHIP_WIRE = ((BF16, BF16), (BF16, BF16), (BF16, BF16))
LIMIT = 24 * 1024 * 1024


def tree_sum(terms):
    terms = list(terms)
    while len(terms) > 1:
        terms = [terms[i] + terms[i + 1] for i in range(0, len(terms), 2)]
    return terms[0]


def put_rows(ref, *values):
    rows = ref.shape[0] - PAD
    parts = []
    for value in values:
        high = value.astype(BF16).astype(F32)
        middle = (value - high).astype(BF16).astype(F32)
        parts += [high, middle, value - high - middle]
    shape = (PAD, ref.shape[1])
    index = lax.broadcasted_iota(jnp.int32, shape, 0)
    block = jnp.zeros(shape, F32)
    for place, part in enumerate(parts):
        block = jnp.where(index == place, jnp.broadcast_to(part, shape), block)
    ref[pl.ds(rows, PAD), :] = block.astype(ref.dtype)


def get_row(ref, which=0):
    rows = ref.shape[0] - PAD
    tail = ref[pl.ds(rows, PAD), :].astype(F32)
    at = 3 * which
    return tail[at : at + 1] + tail[at + 1 : at + 2] + tail[at + 2 : at + 3]


def exponent_of(value):
    return jnp.clip(jnp.floor(jnp.log2(jnp.maximum(value, 1e-36))), -119.0, 119.0)


def put_scaled(ref, exponent, value):
    rows = ref.shape[0] - PAD
    own = exponent_of(value)
    scaled = value * jnp.exp2(-own)
    high = scaled.astype(BF16).astype(F32)
    middle = (scaled - high).astype(BF16).astype(F32)
    parts = [exponent, own, high, 256.0 * middle, 65536.0 * (scaled - high - middle)]
    shape = (PAD, ref.shape[1])
    index = lax.broadcasted_iota(jnp.int32, shape, 0)
    block = jnp.zeros(shape, F32)
    for place, part in enumerate(parts):
        block = jnp.where(index == place, jnp.broadcast_to(part, shape), block)
    ref[pl.ds(rows, PAD), :] = block


def get_scaled(ref):
    rows = ref.shape[0] - PAD
    tail = ref[pl.ds(rows, PAD), :]
    value = tail[2:3] + tail[3:4] * (1.0 / 256.0) + tail[4:5] * (1.0 / 65536.0)
    return jnp.exp2(tail[0:1]), value * jnp.exp2(tail[1:2])


def body_of(ref):
    return ref[pl.ds(0, ref.shape[0] - PAD), :]


def column_sum(values):
    return jnp.sum(values, axis=0, keepdims=True)


def spread(ref, value):
    ref[...] = jnp.broadcast_to(value, ref.shape)


def call(kernel, outs, operands, scratch=()):
    vmem = pl.BlockSpec(memory_space=pltpu.VMEM)
    return pl.pallas_call(
        kernel,
        out_shape=[jax.ShapeDtypeStruct(shape, dtype) for shape, dtype in outs],
        in_specs=[vmem] * len(operands),
        out_specs=[vmem] * len(outs),
        scratch_shapes=scratch,
        compiler_params=pltpu.CompilerParams(vmem_limit_bytes=LIMIT),
    )(*operands)


def shards(states, targets, ridge):
    n_row = lax.axis_size("row")
    n_group = lax.axis_size("group")
    levels = (n_group // 2).bit_length() - 1
    tokens, feats = states.shape
    outs = targets.shape[1]
    feat_share = feats // n_row
    half = tokens // 2
    piece = half // levels
    block = 256
    ridge = ridge.reshape(1, outs)
    scalar = ((8, outs), F32)
    feature_rows = ((feat_share, outs), F32)
    token_rows = ((half, outs), F32)

    def over_row(step, value):
        return lax.ppermute(value, "row", [(i, i ^ step) for i in range(n_row)])

    def over_group(step, value):
        return lax.ppermute(value, "group", [(i, i ^ step) for i in range(n_group)])

    def row_place(step):
        return pl.multiple_of((lax.axis_index("row") ^ step) * feat_share, feat_share)

    def token_place(core_step):
        core = (lax.axis_index("group") % 2) ^ core_step
        return pl.multiple_of(core * half, half)

    def backward(wire, *blocks):
        first = len(blocks) == 1
        wide = 2 * outs if first else outs

        def kernel(a_ref, *refs):
            ins = refs[: len(blocks)]
            own_ref, delta_ref, *msg_refs, vec, prod = refs[len(blocks) :]
            if first:
                whole = ins[0][...]
                high = whole.astype(BF16)
                vec[:, 0:outs] = high
                vec[:, outs:wide] = (whole - high.astype(F32)).astype(BF16)
                delta = jnp.zeros((1, outs), F32)
            else:
                for core_step, ref in enumerate(ins):
                    vec[pl.ds(token_place(core_step), half), :] = body_of(ref)
                delta = get_row(ins[0]) + get_row(ins[1])
            spread(delta_ref, delta)
            turned = vec[...].T
            for start in range(0, feats, block):
                part = jnp.dot(turned, a_ref[:, start : start + block], preferred_element_type=F32)
                if first:
                    part = part[0:outs] + part[outs:wide]
                prod[start : start + block, :] = part.T
            own_ref[...] = prod[pl.ds(row_place(0), feat_share), :]
            if scaled:
                exponent = exponent_of(jnp.max(jnp.abs(prod[...]), axis=0, keepdims=True))
                factor = jnp.exp2(-exponent)
            for step, ref in enumerate(msg_refs, 1):
                part = prod[pl.ds(row_place(step), feat_share), :]
                if scaled:
                    ref[pl.ds(0, feat_share), :] = part * factor
                    put_scaled(ref, exponent, delta)
                else:
                    ref[pl.ds(0, feat_share), :] = part.astype(wire)
                    put_rows(ref, delta)

        scaled = wire == F16
        msgs = [((feat_share + PAD, outs), F32 if scaled else wire)] * (n_row - 1)
        own, delta, *sends = call(
            kernel,
            [feature_rows, scalar] + msgs,
            (states,) + blocks,
            [pltpu.VMEM((tokens, wide), BF16), pltpu.VMEM((feats, outs), F32)],
        )
        got = [over_row(step, send.astype(wire)) for step, send in enumerate(sends, 1)]
        return own, delta, [send.astype(F32) if scaled else send for send in got]

    def begin(own, got):
        def kernel(own_ref, *refs):
            ins, (grad_ref, msg_ref) = refs[: n_row - 1], refs[n_row - 1 :]
            grad = own_ref[...]
            for ref in ins:
                grad = grad + get_scaled(ref)[0] * body_of(ref)
            grad_ref[...] = grad
            msg_ref[pl.ds(0, feat_share), :] = grad.astype(BF16)
            put_rows(msg_ref, column_sum(grad * grad), jnp.zeros((1, outs), F32))

        return call(kernel, [feature_rows, ((feat_share + PAD, outs), BF16)], [own] + got)

    def advance(wire, own, delta, got, gamma, dir_sq, grad, direction, image, weights, residual):
        def kernel(own_ref, delta_ref, *refs):
            ins = refs[: n_row - 1]
            gamma_ref, sq_ref, grad_ref, dir_ref, image_ref, w_ref, r_ref, ridge_ref = refs[n_row - 1 : n_row + 7]
            w_out, r_out, grad_out, msg_ref = refs[n_row + 7 :]
            if wire == F16:
                tails = [get_scaled(ref) for ref in ins]
            else:
                tails = [(1.0, get_row(ref)) for ref in ins]
            image_sq = tree_sum([delta_ref[0:1, :]] + [value for _, value in tails])
            alpha = gamma_ref[0:1, :] / (image_sq + ridge_ref[...] * sq_ref[0:1, :])
            prod = own_ref[...]
            for ref, (scale, _) in zip(ins, tails):
                prod = prod + scale * body_of(ref).astype(F32)
            old_dir = dir_ref[...]
            new = grad_ref[...] - alpha * (prod + ridge_ref[...] * old_dir)
            msg_ref[pl.ds(0, feat_share), :] = new.astype(BF16)
            put_rows(msg_ref, column_sum(new * new), column_sum(new * old_dir))
            grad_out[...] = new
            w_out[...] = w_ref[...] + alpha * old_dir
            r_out[...] = r_ref[...] - alpha * image_ref[...]

        return call(
            kernel,
            [feature_rows, token_rows, feature_rows, ((feat_share + PAD, outs), BF16)],
            [own, delta, *got, gamma, dir_sq, grad, direction, image, weights, residual, ridge],
        )

    def forward(wire, msg):
        blocks = [msg] + [over_row(step, msg) for step in range(1, n_row)]

        def kernel(a_ref, *refs):
            ins = refs[:n_row]
            own_ref, gamma_ref, cross_ref, peer_ref, vec = refs[n_row:]
            for step, ref in enumerate(ins):
                vec[pl.ds(row_place(step), feat_share), :] = body_of(ref)
            gamma = tree_sum([get_row(ref, 0) for ref in ins])
            cross = tree_sum([get_row(ref, 1) for ref in ins])
            spread(gamma_ref, gamma)
            spread(cross_ref, cross)
            for core_step, ref in ((1, peer_ref), (0, own_ref)):
                for start in range(0, half, block):
                    part = jnp.dot(
                        a_ref[pl.ds(pl.multiple_of(token_place(core_step) + start, block), block), :],
                        vec[...],
                        preferred_element_type=F32,
                    )
                    ref[start : start + block, :] = part.astype(ref.dtype)
            put_rows(peer_ref, gamma, cross)

        own, gamma, cross, peer = call(
            kernel,
            [token_rows, scalar, scalar, ((half + PAD, outs), wire)],
            [states] + blocks,
            [pltpu.VMEM((feats, outs), BF16)],
        )
        return own, gamma, cross, over_group(1, peer)

    def pieces(wire):
        return [((piece + (0 if index else PAD), outs), wire) for index in range(levels)]

    def swapped(step, sends):
        return [
            over_group(2 << ((index + step) % levels), send) for index, send in enumerate(sends)
        ]

    def join_cores(wire, own, gamma, cross, got):
        def kernel(own_ref, gamma_ref, cross_ref, got_ref, *msg_refs):
            for index, ref in enumerate(msg_refs):
                place = pl.ds(index * piece, piece)
                both = own_ref[place, :] + got_ref[place, :].astype(F32)
                ref[pl.ds(0, piece), :] = both.astype(wire)
            put_rows(
                msg_refs[0],
                gamma_ref[0:1, :] + get_row(got_ref, 0),
                cross_ref[0:1, :] + get_row(got_ref, 1),
            )

        return call(kernel, pieces(wire), [own, gamma, cross, got])

    def join_chips(wire, sent, got):
        def kernel(*refs):
            mine, theirs, out_refs = refs[:levels], refs[levels : 2 * levels], refs[2 * levels :]
            for ref, own_ref, got_ref in zip(out_refs, mine, theirs):
                place = pl.ds(0, piece)
                both = own_ref[place, :].astype(F32) + got_ref[place, :].astype(F32)
                ref[place, :] = both.astype(wire)
            put_rows(out_refs[0], *[get_row(mine[0], k) + get_row(theirs[0], k) for k in range(2)])

        return call(kernel, pieces(wire), list(sent) + got)

    def image_of(wire, sent, got, grad, before):
        def kernel(*refs):
            mine, theirs = refs[:levels], refs[levels : 2 * levels]
            grad_ref, *rest = refs[2 * levels :]
            gamma_out, sq_out, dir_out, image_out, msg_ref, part_out = rest[-6:]
            gamma, cross = [get_row(mine[0], k) + get_row(theirs[0], k) for k in range(2)]
            spread(gamma_out, gamma)
            direction = grad_ref[...]
            dir_sq = gamma
            if before:
                old_gamma, old_sq, old_dir, old_image = rest[:4]
                beta = gamma / old_gamma[0:1, :]
                direction = direction + beta * old_dir[...]
                dir_sq = gamma + beta * (2.0 * cross + beta * old_sq[0:1, :])
            dir_out[...] = direction
            spread(sq_out, dir_sq)
            image_sq = jnp.zeros((1, outs), F32)
            for index, (own_ref, got_ref) in enumerate(zip(mine, theirs)):
                place = pl.ds(index * piece, piece)
                image = own_ref[pl.ds(0, piece), :].astype(F32) + got_ref[pl.ds(0, piece), :].astype(F32)
                if before:
                    image = image + beta * old_image[place, :]
                image_out[place, :] = image
                msg_ref[place, :] = image.astype(wire)
                image_sq = image_sq + column_sum(image * image)
            put_rows(msg_ref, image_sq)
            spread(part_out, image_sq)

        return call(
            kernel,
            [scalar, scalar, feature_rows, token_rows, ((half + PAD, outs), wire), scalar],
            list(sent) + got + [grad, *before],
        )

    core = lax.axis_index("group") % 2
    weights = jnp.zeros((feat_share, outs), F32)
    residual = lax.dynamic_slice_in_dim(targets, core * half, half, 0)
    own, _, got = backward(ROW_WIRE[0], targets)
    grad, msg = begin(own, got)
    before = ()
    for step in range(ITERS):
        own, gamma, cross, got = forward(CORE_WIRE[step], msg)
        sent = join_cores(CHIP_WIRE[step][0], own, gamma, cross, got)
        got = swapped(0, sent)
        for level in range(1, levels):
            sent = join_chips(CHIP_WIRE[step][1], sent, got)
            got = swapped(level, sent)
        last = step + 1 == ITERS
        gamma, dir_sq, direction, image, msg, part = image_of(
            F32 if last else BF16, sent, got, grad, before
        )
        if not last:
            own, delta, got = backward(ROW_WIRE[step + 1], msg, over_group(1, msg))
            weights, residual, grad, msg = advance(
                ROW_WIRE[step + 1], own, delta, got, gamma, dir_sq, grad, direction, image, weights, residual
            )
            before = (gamma, dir_sq, direction, image)

    def both_cores(own_ref, got_ref, out_ref):
        out_ref[...] = own_ref[...] + got_ref[...]

    (delta,) = call(both_cores, [scalar], [part, over_group(1, part)])
    other_image = over_group(1, image)
    other_residual = over_group(1, residual)
    deltas = [delta] + [over_row(step, delta) for step in range(1, n_row)]

    def finish(*refs):
        delta_refs, refs = refs[:n_row], refs[n_row:]
        gamma_ref, sq_ref, ridge_ref, image_ref, other_image_ref, r_ref, other_r_ref, dir_ref, w_ref, w_out, r_out = refs
        image_sq = tree_sum([ref[0:1, :] for ref in delta_refs])
        alpha = gamma_ref[0:1, :] / (image_sq + ridge_ref[...] * sq_ref[0:1, :])
        w_out[...] = w_ref[...] + alpha * dir_ref[...]
        r_out[pl.ds(token_place(0), half), :] = r_ref[...] - alpha * image_ref[...]
        r_out[pl.ds(token_place(1), half), :] = other_r_ref[...] - alpha * other_image_ref[...]

    weights, residual = call(
        finish,
        [feature_rows, ((tokens, outs), F32)],
        [*deltas, gamma, dir_sq, ridge, image, other_image, residual, other_residual, direction, weights],
    )
    return weights, residual


def solution(mesh):
    placed = (P("row", "group"), P("row", None), P())
    return jax.shard_map(
        shards,
        mesh=mesh,
        in_specs=placed,
        out_specs=(P(("group", "row"), None), P("row", None)),
        check_vma=False,
    )
```

```python
import jax
import jax.numpy as jnp
from jax import lax
from jax.experimental import pallas as pl
from jax.experimental.pallas import tpu as pltpu
from jax.sharding import PartitionSpec as P

ITERS = 3
PAD = 16
F32 = jnp.float32
BF16 = jnp.bfloat16
F16 = jnp.float16
ROW_WIRE = (F16, F16, BF16)
CORE_WIRE = (F32, F32, F32)
CHIP_WIRE = ((BF16, BF16), (BF16, BF16), (BF16, BF16))
FIRST_PIECE = 9
ROW_ORDER = 1
LIMIT = 24 * 1024 * 1024


def tree_sum(terms):
    terms = list(terms)
    while len(terms) > 1:
        terms = [terms[i] + terms[i + 1] for i in range(0, len(terms), 2)]
    return terms[0]


def put_rows(ref, *values):
    rows = ref.shape[0] - PAD
    parts = []
    for value in values:
        high = value.astype(BF16).astype(F32)
        middle = (value - high).astype(BF16).astype(F32)
        parts += [high, middle, value - high - middle]
    shape = (PAD, ref.shape[1])
    index = lax.broadcasted_iota(jnp.int32, shape, 0)
    block = jnp.zeros(shape, F32)
    for place, part in enumerate(parts):
        block = jnp.where(index == place, jnp.broadcast_to(part, shape), block)
    ref[pl.ds(rows, PAD), :] = block.astype(ref.dtype)


def get_row(ref, which=0):
    rows = ref.shape[0] - PAD
    tail = ref[pl.ds(rows, PAD), :].astype(F32)
    at = 3 * which
    return tail[at : at + 1] + tail[at + 1 : at + 2] + tail[at + 2 : at + 3]


def exponent_of(value):
    return jnp.clip(jnp.floor(jnp.log2(jnp.maximum(value, 1e-36))), -119.0, 119.0)


def put_scaled(ref, exponent, value):
    rows = ref.shape[0] - PAD
    own = exponent_of(value)
    scaled = value * jnp.exp2(-own)
    high = scaled.astype(BF16).astype(F32)
    middle = (scaled - high).astype(BF16).astype(F32)
    parts = [exponent, own, high, 256.0 * middle, 65536.0 * (scaled - high - middle)]
    shape = (PAD, ref.shape[1])
    index = lax.broadcasted_iota(jnp.int32, shape, 0)
    block = jnp.zeros(shape, F32)
    for place, part in enumerate(parts):
        block = jnp.where(index == place, jnp.broadcast_to(part, shape), block)
    ref[pl.ds(rows, PAD), :] = block


def get_scaled(ref):
    rows = ref.shape[0] - PAD
    tail = ref[pl.ds(rows, PAD), :]
    value = tail[2:3] + tail[3:4] * (1.0 / 256.0) + tail[4:5] * (1.0 / 65536.0)
    return jnp.exp2(tail[0:1]), value * jnp.exp2(tail[1:2])


def body_of(ref):
    return ref[pl.ds(0, ref.shape[0] - PAD), :]


def column_sum(values):
    return jnp.sum(values, axis=0, keepdims=True)


def spread(ref, value):
    ref[...] = jnp.broadcast_to(value, ref.shape)


def call(kernel, outs, operands, scratch=()):
    vmem = pl.BlockSpec(memory_space=pltpu.VMEM)
    return pl.pallas_call(
        kernel,
        out_shape=[jax.ShapeDtypeStruct(shape, dtype) for shape, dtype in outs],
        in_specs=[vmem] * len(operands),
        out_specs=[vmem] * len(outs),
        scratch_shapes=scratch,
        compiler_params=pltpu.CompilerParams(vmem_limit_bytes=LIMIT),
    )(*operands)


def shards(states, targets, ridge):
    n_row = lax.axis_size("row")
    n_group = lax.axis_size("group")
    levels = (n_group // 2).bit_length() - 1
    tokens, feats = states.shape
    outs = targets.shape[1]
    feat_share = feats // n_row
    half = tokens // 2
    piece_rows = [half // levels] * levels
    if levels == 2:
        piece_rows = [half * FIRST_PIECE // 16, half - half * FIRST_PIECE // 16]
    piece_starts = [sum(piece_rows[:index]) for index in range(levels)]
    row_steps = list(range(1, n_row))[::ROW_ORDER]
    block = 256
    ridge = ridge.reshape(1, outs)
    scalar = ((8, outs), F32)
    feature_rows = ((feat_share, outs), F32)
    token_rows = ((half, outs), F32)

    def over_row(step, value):
        return lax.ppermute(value, "row", [(i, i ^ step) for i in range(n_row)])

    def over_group(step, value):
        return lax.ppermute(value, "group", [(i, i ^ step) for i in range(n_group)])

    def row_place(step):
        return pl.multiple_of((lax.axis_index("row") ^ step) * feat_share, feat_share)

    def token_place(core_step):
        core = (lax.axis_index("group") % 2) ^ core_step
        return pl.multiple_of(core * half, half)

    def cut(wire, prod, delta, own_ref, msg_refs):
        own_ref[...] = prod[pl.ds(row_place(0), feat_share), :]
        if wire == F16:
            exponent = exponent_of(jnp.max(jnp.abs(prod[...]), axis=0, keepdims=True))
            factor = jnp.exp2(-exponent)
        for step, ref in zip(row_steps, msg_refs):
            part = prod[pl.ds(row_place(step), feat_share), :]
            if wire == F16:
                ref[pl.ds(0, feat_share), :] = part * factor
                put_scaled(ref, exponent, delta)
            else:
                ref[pl.ds(0, feat_share), :] = part.astype(wire)
                put_rows(ref, delta)

    def cut_shapes(wire):
        return [((feat_share + PAD, outs), F32 if wire == F16 else wire)] * (n_row - 1)

    def scattered(wire, sends):
        got = {step: over_row(step, send.astype(wire)) for step, send in zip(row_steps, sends)}
        got = [got[step] for step in range(1, n_row)]
        return [send.astype(F32) if wire == F16 else send for send in got]

    def backward_first(wire):
        def split(t_ref, turned_ref, r_out):
            for start in range(0, tokens, block):
                whole = t_ref[start : start + block, :]
                high = whole.astype(BF16)
                turned_ref[0:outs, start : start + block] = high.T
                turned_ref[outs : 2 * outs, start : start + block] = (whole - high.astype(F32)).astype(BF16).T
            r_out[...] = t_ref[pl.ds(token_place(0), half), :]

        def product(a_ref, turned_ref, own_ref, *refs):
            *msg_refs, prod = refs
            for start in range(0, feats, block):
                cols = slice(start, start + block)
                part = jnp.dot(turned_ref[...], a_ref[:, cols], preferred_element_type=F32)
                prod[cols, :] = (part[0:outs] + part[outs : 2 * outs]).T
            cut(wire, prod, jnp.zeros((1, outs), F32), own_ref, msg_refs)

        turned, residual = call(split, [((2 * outs, tokens), BF16), token_rows], [targets])
        own, *sends = call(
            product,
            [feature_rows] + cut_shapes(wire),
            [states, turned],
            [pltpu.VMEM((feats, outs), F32)],
        )
        return residual, own, scattered(wire, sends)

    def backward(wire, mine, theirs):
        def half_product(a_ref, ref, core_step, cols):
            return jnp.dot(
                body_of(ref).T,
                a_ref[pl.ds(token_place(core_step), half), cols],
                preferred_element_type=F32,
            )

        def first_half(a_ref, mine_ref, part_ref):
            for start in range(0, feats, block):
                cols = slice(start, start + block)
                part_ref[:, cols] = half_product(a_ref, mine_ref, 0, cols)

        def second_half(a_ref, mine_ref, theirs_ref, part_ref, own_ref, delta_ref, *refs):
            *msg_refs, prod = refs
            delta = get_row(mine_ref) + get_row(theirs_ref)
            spread(delta_ref, delta)
            for start in range(0, feats, block):
                cols = slice(start, start + block)
                prod[cols, :] = (part_ref[:, cols] + half_product(a_ref, theirs_ref, 1, cols)).T
            cut(wire, prod, delta, own_ref, msg_refs)

        (part,) = call(first_half, [((outs, feats), F32)], [states, mine])
        own, delta, *sends = call(
            second_half,
            [feature_rows, scalar] + cut_shapes(wire),
            [states, mine, theirs, part],
            [pltpu.VMEM((feats, outs), F32)],
        )
        return own, delta, scattered(wire, sends)

    def begin(own, got):
        def kernel(own_ref, *refs):
            ins, (grad_ref, msg_ref) = refs[: n_row - 1], refs[n_row - 1 :]
            grad = own_ref[...]
            for ref in ins:
                grad = grad + get_scaled(ref)[0] * body_of(ref)
            grad_ref[...] = grad
            msg_ref[pl.ds(0, feat_share), :] = grad.astype(BF16)
            put_rows(msg_ref, column_sum(grad * grad), jnp.zeros((1, outs), F32))

        return call(kernel, [feature_rows, ((feat_share + PAD, outs), BF16)], [own] + got)

    def advance(wire, own, delta, got, gamma, dir_sq, grad, direction, image, weights, residual):
        def kernel(own_ref, delta_ref, *refs):
            ins = refs[: n_row - 1]
            gamma_ref, sq_ref, grad_ref, dir_ref, image_ref, r_ref, ridge_ref = refs[n_row - 1 : n_row + 6]
            *w_ref, w_out, r_out, grad_out, msg_ref = refs[n_row + 6 :]
            if wire == F16:
                tails = [get_scaled(ref) for ref in ins]
            else:
                tails = [(1.0, get_row(ref)) for ref in ins]
            image_sq = tree_sum([delta_ref[0:1, :]] + [value for _, value in tails])
            alpha = gamma_ref[0:1, :] / (image_sq + ridge_ref[...] * sq_ref[0:1, :])
            prod = own_ref[...]
            for ref, (scale, _) in zip(ins, tails):
                prod = prod + scale * body_of(ref).astype(F32)
            old_dir = dir_ref[...]
            new = grad_ref[...] - alpha * (prod + ridge_ref[...] * old_dir)
            msg_ref[pl.ds(0, feat_share), :] = new.astype(BF16)
            put_rows(msg_ref, column_sum(new * new), column_sum(new * old_dir))
            grad_out[...] = new
            step_taken = alpha * old_dir
            w_out[...] = w_ref[0][...] + step_taken if w_ref else step_taken
            r_out[...] = r_ref[...] - alpha * image_ref[...]

        return call(
            kernel,
            [feature_rows, token_rows, feature_rows, ((feat_share + PAD, outs), BF16)],
            [own, delta, *got, gamma, dir_sq, grad, direction, image, residual, ridge, *weights],
        )

    def forward(wire, msg):
        got = {step: over_row(step, msg) for step in row_steps}
        blocks = [msg] + [got[step] for step in range(1, n_row)]

        def half_product(a_ref, vec, core_step, ref):
            for start in range(0, half, block):
                part = jnp.dot(
                    a_ref[pl.ds(pl.multiple_of(token_place(core_step) + start, block), block), :],
                    vec[...],
                    preferred_element_type=F32,
                )
                ref[start : start + block, :] = part.astype(ref.dtype)

        def first_half(a_ref, *refs):
            ins = refs[:n_row]
            peer_ref, gamma_ref, cross_ref, vec = refs[n_row:]
            for step, ref in enumerate(ins):
                vec[pl.ds(row_place(step), feat_share), :] = body_of(ref)
            gamma = tree_sum([get_row(ref, 0) for ref in ins])
            cross = tree_sum([get_row(ref, 1) for ref in ins])
            spread(gamma_ref, gamma)
            spread(cross_ref, cross)
            half_product(a_ref, vec, 1, peer_ref)
            put_rows(peer_ref, gamma, cross)

        def second_half(a_ref, vec, own_ref):
            half_product(a_ref, vec, 0, own_ref)

        peer, gamma, cross, vec = call(
            first_half,
            [((half + PAD, outs), wire), scalar, scalar, ((feats, outs), BF16)],
            [states] + blocks,
        )
        got = over_group(1, peer)
        (own,) = call(second_half, [token_rows], [states, vec])
        return own, gamma, cross, got

    def pieces(wire):
        return [((rows + (0 if index else PAD), outs), wire) for index, rows in enumerate(piece_rows)]

    def swapped(step, sends):
        return [
            over_group(2 << ((index + step) % levels), send) for index, send in enumerate(sends)
        ]

    def join_cores(wire, own, gamma, cross, got):
        def kernel(own_ref, gamma_ref, cross_ref, got_ref, *msg_refs):
            for index, ref in enumerate(msg_refs):
                place = pl.ds(piece_starts[index], piece_rows[index])
                both = own_ref[place, :] + got_ref[place, :].astype(F32)
                ref[pl.ds(0, piece_rows[index]), :] = both.astype(wire)
            put_rows(
                msg_refs[0],
                gamma_ref[0:1, :] + get_row(got_ref, 0),
                cross_ref[0:1, :] + get_row(got_ref, 1),
            )

        return call(kernel, pieces(wire), [own, gamma, cross, got])

    def join_chips(wire, sent, got):
        def kernel(*refs):
            mine, theirs, out_refs = refs[:levels], refs[levels : 2 * levels], refs[2 * levels :]
            for ref, own_ref, got_ref, rows in zip(out_refs, mine, theirs, piece_rows):
                place = pl.ds(0, rows)
                both = own_ref[place, :].astype(F32) + got_ref[place, :].astype(F32)
                ref[place, :] = both.astype(wire)
            put_rows(out_refs[0], *[get_row(mine[0], k) + get_row(theirs[0], k) for k in range(2)])

        return call(kernel, pieces(wire), list(sent) + got)

    def image_of(last, sent, got, grad, before):
        def kernel(*refs):
            mine, theirs = refs[:levels], refs[levels : 2 * levels]
            grad_ref, *rest = refs[2 * levels :]
            gamma_out, sq_out, dir_out, image_out, sum_out = rest[-5:]
            gamma, cross = [get_row(mine[0], k) + get_row(theirs[0], k) for k in range(2)]
            spread(gamma_out, gamma)
            direction = grad_ref[...]
            dir_sq = gamma
            if before:
                old_gamma, old_sq, old_dir, old_image = rest[:4]
                beta = gamma / old_gamma[0:1, :]
                direction = direction + beta * old_dir[...]
                dir_sq = gamma + beta * (2.0 * cross + beta * old_sq[0:1, :])
            dir_out[...] = direction
            spread(sq_out, dir_sq)
            image_sq = jnp.zeros((1, outs), F32)
            for index, (own_ref, got_ref) in enumerate(zip(mine, theirs)):
                place = pl.ds(piece_starts[index], piece_rows[index])
                there = pl.ds(0, piece_rows[index])
                image = own_ref[there, :].astype(F32) + got_ref[there, :].astype(F32)
                if before:
                    image = image + beta * old_image[place, :]
                image_out[place, :] = image
                if not last:
                    sum_out[place, :] = image.astype(BF16)
                image_sq = image_sq + column_sum(image * image)
            if last:
                spread(sum_out, image_sq)
            else:
                put_rows(sum_out, image_sq)

        return call(
            kernel,
            [scalar, scalar, feature_rows, token_rows, scalar if last else ((half + PAD, outs), BF16)],
            list(sent) + got + [grad, *before],
        )

    weights = ()
    residual, own, got = backward_first(ROW_WIRE[0])
    grad, msg = begin(own, got)
    before = ()
    for step in range(ITERS):
        own, gamma, cross, got = forward(CORE_WIRE[step], msg)
        sent = join_cores(CHIP_WIRE[step][0], own, gamma, cross, got)
        got = swapped(0, sent)
        for level in range(1, levels):
            sent = join_chips(CHIP_WIRE[step][1], sent, got)
            got = swapped(level, sent)
        last = step + 1 == ITERS
        gamma, dir_sq, direction, image, msg = image_of(last, sent, got, grad, before)
        if not last:
            own, delta, got = backward(ROW_WIRE[step + 1], msg, over_group(1, msg))
            new, residual, grad, msg = advance(
                ROW_WIRE[step + 1], own, delta, got, gamma, dir_sq, grad, direction, image, weights, residual
            )
            weights = (new,)
            before = (gamma, dir_sq, direction, image)

    def both_cores(own_ref, got_ref, image_ref, out_ref, same_image_ref):
        out_ref[...] = own_ref[...] + got_ref[...]

    vmem, anywhere = pl.BlockSpec(memory_space=pltpu.VMEM), pl.BlockSpec(memory_space=pl.ANY)
    delta, image = pl.pallas_call(
        both_cores,
        out_shape=[jax.ShapeDtypeStruct(*scalar), jax.ShapeDtypeStruct(*token_rows)],
        in_specs=[vmem, vmem, anywhere],
        out_specs=[vmem, anywhere],
        input_output_aliases={2: 1},
        compiler_params=pltpu.CompilerParams(vmem_limit_bytes=LIMIT),
    )(msg, over_group(1, msg), image)
    other_image = over_group(1, image)
    other_residual = over_group(1, residual)
    got = {step: over_row(step, delta) for step in row_steps}
    deltas = [delta] + [got[step] for step in range(1, n_row)]

    def finish(*refs):
        delta_refs, refs = refs[:n_row], refs[n_row:]
        gamma_ref, sq_ref, ridge_ref, image_ref, other_image_ref, r_ref, other_r_ref, dir_ref, w_ref, w_out, r_out = refs
        image_sq = tree_sum([ref[0:1, :] for ref in delta_refs])
        alpha = gamma_ref[0:1, :] / (image_sq + ridge_ref[...] * sq_ref[0:1, :])
        w_out[...] = w_ref[...] + alpha * dir_ref[...]
        r_out[pl.ds(token_place(0), half), :] = r_ref[...] - alpha * image_ref[...]
        r_out[pl.ds(token_place(1), half), :] = other_r_ref[...] - alpha * other_image_ref[...]

    weights, residual = call(
        finish,
        [feature_rows, ((tokens, outs), F32)],
        [*deltas, gamma, dir_sq, ridge, image, other_image, residual, other_residual, direction, *weights],
    )
    return weights, residual


def solution(mesh):
    placed = (P("row", "group"), P("row", None), P())
    return jax.shard_map(
        shards,
        mesh=mesh,
        in_specs=placed,
        out_specs=(P(("group", "row"), None), P("row", None)),
        check_vma=False,
    )
```

```python
import functools

import jax
import jax.numpy as jnp
from jax import lax
from jax.experimental import pallas as pl
from jax.experimental.pallas import tpu as pltpu
from jax.sharding import PartitionSpec as P

ITERS = 3
PAD = 16
F32 = jnp.float32
BF16 = jnp.bfloat16
F16 = jnp.float16
ROW_WIRE = (F16, F16, BF16)
CORE_WIRE = (F32, F32, F32)
CHIP_WIRE = ((BF16, BF16), (BF16, BF16), (BF16, BF16))
FIRST_PIECE = 9
ROW_ORDER = 1
LIMIT = 24 * 1024 * 1024


def tree_sum(terms):
    terms = list(terms)
    while len(terms) > 1:
        terms = [terms[i] + terms[i + 1] for i in range(0, len(terms), 2)]
    return terms[0]


def put_rows(ref, *values):
    rows = ref.shape[0] - PAD
    parts = []
    for value in values:
        high = value.astype(BF16).astype(F32)
        middle = (value - high).astype(BF16).astype(F32)
        parts += [high, middle, value - high - middle]
    shape = (PAD, ref.shape[1])
    index = lax.broadcasted_iota(jnp.int32, shape, 0)
    block = jnp.zeros(shape, F32)
    for place, part in enumerate(parts):
        block = jnp.where(index == place, jnp.broadcast_to(part, shape), block)
    ref[pl.ds(rows, PAD), :] = block.astype(ref.dtype)


def get_row(ref, which=0):
    rows = ref.shape[0] - PAD
    tail = ref[pl.ds(rows, PAD), :].astype(F32)
    at = 3 * which
    return tail[at : at + 1] + tail[at + 1 : at + 2] + tail[at + 2 : at + 3]


def exponent_of(value):
    return jnp.clip(jnp.floor(jnp.log2(jnp.maximum(value, 1e-36))), -119.0, 119.0)


def put_scaled(ref, exponent, value):
    rows = ref.shape[0] - PAD
    own = exponent_of(value)
    scaled = value * jnp.exp2(-own)
    high = scaled.astype(BF16).astype(F32)
    middle = (scaled - high).astype(BF16).astype(F32)
    parts = [exponent, own, high, 256.0 * middle, 65536.0 * (scaled - high - middle)]
    shape = (PAD, ref.shape[1])
    index = lax.broadcasted_iota(jnp.int32, shape, 0)
    block = jnp.zeros(shape, F32)
    for place, part in enumerate(parts):
        block = jnp.where(index == place, jnp.broadcast_to(part, shape), block)
    ref[pl.ds(rows, PAD), :] = block


def get_scaled(ref):
    rows = ref.shape[0] - PAD
    tail = ref[pl.ds(rows, PAD), :]
    value = tail[2:3] + tail[3:4] * (1.0 / 256.0) + tail[4:5] * (1.0 / 65536.0)
    return jnp.exp2(tail[0:1]), value * jnp.exp2(tail[1:2])


def body_of(ref):
    return ref[pl.ds(0, ref.shape[0] - PAD), :]


def column_sum(values):
    return jnp.sum(values, axis=0, keepdims=True)


def spread(ref, value):
    ref[...] = jnp.broadcast_to(value, ref.shape)


def call(kernel, outs, operands, scratch=()):
    vmem = pl.BlockSpec(memory_space=pltpu.VMEM)
    return pl.pallas_call(
        kernel,
        out_shape=[jax.ShapeDtypeStruct(shape, dtype) for shape, dtype in outs],
        in_specs=[vmem] * len(operands),
        out_specs=[vmem] * len(outs),
        scratch_shapes=scratch,
        compiler_params=pltpu.CompilerParams(vmem_limit_bytes=LIMIT),
    )(*operands)


def shards(states, targets, ridge):
    n_row = lax.axis_size("row")
    n_group = lax.axis_size("group")
    levels = (n_group // 2).bit_length() - 1
    tokens, feats = states.shape
    outs = targets.shape[1]
    feat_share = feats // n_row
    half = tokens // 2
    piece_rows = [half // levels] * levels
    if levels == 2:
        piece_rows = [half * FIRST_PIECE // 16, half - half * FIRST_PIECE // 16]
    piece_starts = [sum(piece_rows[:index]) for index in range(levels)]
    row_steps = list(range(1, n_row))[::ROW_ORDER]
    block = 256
    ridge = ridge.reshape(1, outs)
    scalar = ((8, outs), F32)
    feature_rows = ((feat_share, outs), F32)
    token_rows = ((half, outs), F32)

    def over_row(step, value):
        return lax.ppermute(value, "row", [(i, i ^ step) for i in range(n_row)])

    def over_group(step, value):
        return lax.ppermute(value, "group", [(i, i ^ step) for i in range(n_group)])

    def row_place(step):
        return pl.multiple_of((lax.axis_index("row") ^ step) * feat_share, feat_share)

    def token_place(core_step):
        core = (lax.axis_index("group") % 2) ^ core_step
        return pl.multiple_of(core * half, half)

    def cut(wire, prod, delta, own_ref, msg_refs):
        own_ref[...] = prod[pl.ds(row_place(0), feat_share), :]
        if wire == F16:
            exponent = exponent_of(jnp.max(jnp.abs(prod[...]), axis=0, keepdims=True))
            factor = jnp.exp2(-exponent)
        for step, ref in zip(row_steps, msg_refs):
            part = prod[pl.ds(row_place(step), feat_share), :]
            if wire == F16:
                ref[pl.ds(0, feat_share), :] = part * factor
                put_scaled(ref, exponent, delta)
            else:
                ref[pl.ds(0, feat_share), :] = part.astype(wire)
                put_rows(ref, delta)

    def cut_shapes(wire):
        return [((feat_share + PAD, outs), F32 if wire == F16 else wire)] * (n_row - 1)

    def scattered(wire, sends):
        got = {step: over_row(step, send.astype(wire)) for step, send in zip(row_steps, sends)}
        got = [got[step] for step in range(1, n_row)]
        return [send.astype(F32) if wire == F16 else send for send in got]

    def backward_first(wire):
        def split(t_ref, turned_ref, r_out):
            for start in range(0, tokens, block):
                whole = t_ref[start : start + block, :]
                high = whole.astype(BF16)
                turned_ref[0:outs, start : start + block] = high.T
                turned_ref[outs : 2 * outs, start : start + block] = (whole - high.astype(F32)).astype(BF16).T
            r_out[...] = t_ref[pl.ds(token_place(0), half), :]

        def product(a_ref, turned_ref, own_ref, *refs):
            *msg_refs, prod = refs
            for start in range(0, feats, block):
                cols = slice(start, start + block)
                part = jnp.dot(turned_ref[...], a_ref[:, cols], preferred_element_type=F32)
                prod[cols, :] = (part[0:outs] + part[outs : 2 * outs]).T
            cut(wire, prod, jnp.zeros((1, outs), F32), own_ref, msg_refs)

        turned, residual = call(split, [((2 * outs, tokens), BF16), token_rows], [targets])
        own, *sends = call(
            product,
            [feature_rows] + cut_shapes(wire),
            [states, turned],
            [pltpu.VMEM((feats, outs), F32)],
        )
        return residual, own, scattered(wire, sends)

    def backward(wire, mine, theirs):
        def half_product(a_ref, refs, core_step, cols):
            total = None
            for ref, start, rows in zip(refs, piece_starts, piece_rows):
                place = pl.ds(pl.multiple_of(token_place(core_step) + start, 64), rows)
                part = jnp.dot(ref[pl.ds(0, rows), :].T, a_ref[place, cols], preferred_element_type=F32)
                total = part if total is None else total + part
            return total

        def first_half(a_ref, *refs):
            *mine_refs, part_ref = refs
            for start in range(0, feats, block):
                cols = slice(start, start + block)
                part_ref[:, cols] = half_product(a_ref, mine_refs, 0, cols)

        def second_half(a_ref, *refs):
            mine_ref, theirs_refs = refs[0], refs[1 : levels + 1]
            part_ref, own_ref, delta_ref, *msg_refs, prod = refs[levels + 1 :]
            delta = get_row(mine_ref) + get_row(theirs_refs[-1])
            spread(delta_ref, delta)
            for start in range(0, feats, block):
                cols = slice(start, start + block)
                prod[cols, :] = (part_ref[:, cols] + half_product(a_ref, theirs_refs, 1, cols)).T
            cut(wire, prod, delta, own_ref, msg_refs)

        (part,) = call(first_half, [((outs, feats), F32)], [states, *mine])
        own, delta, *sends = call(
            second_half,
            [feature_rows, scalar] + cut_shapes(wire),
            [states, mine[-1], *theirs, part],
            [pltpu.VMEM((feats, outs), F32)],
        )
        return own, delta, scattered(wire, sends)

    def begin(own, got):
        def kernel(own_ref, *refs):
            ins, (grad_ref, msg_ref) = refs[: n_row - 1], refs[n_row - 1 :]
            grad = own_ref[...]
            for ref in ins:
                grad = grad + get_scaled(ref)[0] * body_of(ref)
            grad_ref[...] = grad
            msg_ref[pl.ds(0, feat_share), :] = grad.astype(BF16)
            put_rows(msg_ref, column_sum(grad * grad), jnp.zeros((1, outs), F32))

        return call(kernel, [feature_rows, ((feat_share + PAD, outs), BF16)], [own] + got)

    def advance(wire, own, delta, got, gamma, dir_sq, grad, direction, images, weights, residual):
        def kernel(own_ref, delta_ref, *refs):
            ins = refs[: n_row - 1]
            gamma_ref, sq_ref, grad_ref, dir_ref, r_ref, ridge_ref = refs[n_row - 1 : n_row + 5]
            image_refs = refs[n_row + 5 : n_row + 5 + levels]
            *w_ref, w_out, r_out, grad_out, msg_ref = refs[n_row + 5 + levels :]
            if wire == F16:
                tails = [get_scaled(ref) for ref in ins]
            else:
                tails = [(1.0, get_row(ref)) for ref in ins]
            image_sq = tree_sum([delta_ref[0:1, :]] + [value for _, value in tails])
            alpha = gamma_ref[0:1, :] / (image_sq + ridge_ref[...] * sq_ref[0:1, :])
            prod = own_ref[...]
            for ref, (scale, _) in zip(ins, tails):
                prod = prod + scale * body_of(ref).astype(F32)
            old_dir = dir_ref[...]
            new = grad_ref[...] - alpha * (prod + ridge_ref[...] * old_dir)
            msg_ref[pl.ds(0, feat_share), :] = new.astype(BF16)
            put_rows(msg_ref, column_sum(new * new), column_sum(new * old_dir))
            grad_out[...] = new
            step_taken = alpha * old_dir
            w_out[...] = w_ref[0][...] + step_taken if w_ref else step_taken
            for ref, start, rows in zip(image_refs, piece_starts, piece_rows):
                place = pl.ds(start, rows)
                r_out[place, :] = r_ref[place, :] - alpha * ref[...]

        return call(
            kernel,
            [feature_rows, token_rows, feature_rows, ((feat_share + PAD, outs), BF16)],
            [own, delta, *got, gamma, dir_sq, grad, direction, residual, ridge, *images, *weights],
        )

    def forward(wire, msg):
        got = {step: over_row(step, msg) for step in row_steps}
        blocks = [msg] + [got[step] for step in range(1, n_row)]

        def product(a_ref, vec, core_step, index, ref):
            start, rows = piece_starts[index], piece_rows[index]
            place = pl.ds(pl.multiple_of(token_place(core_step) + start, 64), rows)
            part = jnp.dot(a_ref[place, :], vec[...], preferred_element_type=F32)
            ref[pl.ds(0, rows), :] = part.astype(ref.dtype)

        def first_piece(a_ref, *refs):
            ins = refs[:n_row]
            peer_ref, gamma_ref, cross_ref, vec = refs[n_row:]
            for step, ref in enumerate(ins):
                vec[pl.ds(row_place(step), feat_share), :] = body_of(ref)
            gamma = tree_sum([get_row(ref, 0) for ref in ins])
            cross = tree_sum([get_row(ref, 1) for ref in ins])
            spread(gamma_ref, gamma)
            spread(cross_ref, cross)
            product(a_ref, vec, 1, 0, peer_ref)
            put_rows(peer_ref, gamma, cross)

        def later_piece(index, a_ref, vec, peer_ref):
            product(a_ref, vec, 1, index, peer_ref)

        def own_pieces(a_ref, vec, *refs):
            for index, ref in enumerate(refs):
                product(a_ref, vec, 0, index, ref)

        peer, gamma, cross, vec = call(
            first_piece,
            [pieces(wire)[0], scalar, scalar, ((feats, outs), BF16)],
            [states] + blocks,
        )
        got = [over_group(1, peer)]
        for index in range(1, levels):
            (peer,) = call(functools.partial(later_piece, index), [pieces(wire)[index]], [states, vec])
            got.append(over_group(1, peer))
        own = call(own_pieces, [((rows, outs), F32) for rows in piece_rows], [states, vec])
        return own, gamma, cross, got

    def pieces(wire):
        return [((rows + (0 if index else PAD), outs), wire) for index, rows in enumerate(piece_rows)]

    def swapped(step, sends):
        return [
            over_group(2 << ((index + step) % levels), send) for index, send in enumerate(sends)
        ]

    def join_cores(wire, own, gamma, cross, got):
        def kernel(own_ref, got_ref, *refs):
            *scalars, out_ref = refs
            place = pl.ds(0, own_ref.shape[0])
            out_ref[place, :] = (own_ref[...] + got_ref[place, :].astype(F32)).astype(wire)
            if scalars:
                put_rows(out_ref, *[ref[0:1, :] + get_row(got_ref, k) for k, ref in enumerate(scalars)])

        return [
            call(kernel, [shape], [own[index], got[index]] + ([] if index else [gamma, cross]))[0]
            for index, shape in enumerate(pieces(wire))
        ]

    def join_chips(wire, sent, got):
        def kernel(has_scalars, rows, own_ref, got_ref, out_ref):
            place = pl.ds(0, rows)
            both = own_ref[place, :].astype(F32) + got_ref[place, :].astype(F32)
            out_ref[place, :] = both.astype(wire)
            if has_scalars:
                put_rows(out_ref, *[get_row(own_ref, k) + get_row(got_ref, k) for k in range(2)])

        return [
            call(functools.partial(kernel, index == 0, piece_rows[index]), [shape], [sent[index], got[index]])[0]
            for index, shape in enumerate(pieces(wire))
        ]

    def image_of(last, sent, got, grad, before):
        def first_piece(own_ref, got_ref, grad_ref, *refs):
            old, (gamma_out, beta_out, sq_out, dir_out, *outputs) = refs[:-6 - more], refs[-6 - more :]
            gamma, cross = [get_row(own_ref, k) + get_row(got_ref, k) for k in range(2)]
            spread(gamma_out, gamma)
            direction = grad_ref[...]
            dir_sq = gamma
            beta = None
            if before:
                old_gamma, old_sq, old_dir = old[:3]
                beta = gamma / old_gamma[0:1, :]
                direction = direction + beta * old_dir[...]
                dir_sq = gamma + beta * (2.0 * cross + beta * old_sq[0:1, :])
                spread(beta_out, beta)
            else:
                spread(beta_out, gamma)
            dir_out[...] = direction
            spread(sq_out, dir_sq)
            part = piece_image(0, own_ref, got_ref, beta, old[3:], outputs)
            spread(outputs[-1], part)

        def later_piece(index, own_ref, got_ref, part_ref, beta_ref, *refs):
            count = len(shapes(index))
            old, outputs = refs[:-count], refs[-count:]
            part = part_ref[0:1, :] + piece_image(index, own_ref, got_ref, beta_ref[0:1, :], old, outputs)
            if not last and index + 1 == levels:
                put_rows(outputs[1], part)
            else:
                spread(outputs[-1], part)

        def piece_image(index, own_ref, got_ref, beta, old, outputs):
            place = pl.ds(0, piece_rows[index])
            image = own_ref[place, :].astype(F32) + got_ref[place, :].astype(F32)
            if before:
                image = image + beta * old[0][...]
            outputs[0][...] = image
            if not last:
                outputs[1][place, :] = image.astype(BF16)
            return column_sum(image * image)

        more = 0 if last else 1

        def shapes(index):
            rows = piece_rows[index]
            tail = PAD if index + 1 == levels else 0
            shape = [((rows, outs), F32)] + [((rows + tail, outs), BF16)] * more
            return shape + [scalar] if last or index + 1 < levels else shape

        gamma, beta, dir_sq, direction, image, *msg, part = call(
            first_piece,
            [scalar, scalar, scalar, feature_rows] + shapes(0),
            [sent[0], got[0], grad] + list(before[:3]) + list(before[3][:1] if before else ()),
        )
        images, msgs = [image], msg
        for index in range(1, levels):
            image, *msg = call(
                functools.partial(later_piece, index),
                shapes(index),
                [sent[index], got[index], part, beta] + list(before[3][index : index + 1] if before else ()),
            )
            if last or index + 1 < levels:
                *msg, part = msg
            images.append(image)
            msgs += msg
        return gamma, dir_sq, direction, images, msgs, part

    weights = ()
    residual, own, got = backward_first(ROW_WIRE[0])
    grad, msg = begin(own, got)
    before = ()
    for step in range(ITERS):
        own, gamma, cross, got = forward(CORE_WIRE[step], msg)
        sent = join_cores(CHIP_WIRE[step][0], own, gamma, cross, got)
        got = swapped(0, sent)
        for level in range(1, levels):
            sent = join_chips(CHIP_WIRE[step][1], sent, got)
            got = swapped(level, sent)
        last = step + 1 == ITERS
        gamma, dir_sq, direction, images, msgs, part = image_of(last, sent, got, grad, before)
        if not last:
            own, delta, got = backward(
                ROW_WIRE[step + 1], msgs, [over_group(1, msg) for msg in msgs]
            )
            new, residual, grad, msg = advance(
                ROW_WIRE[step + 1], own, delta, got, gamma, dir_sq, grad, direction, images, weights, residual
            )
            weights = (new,)
            before = (gamma, dir_sq, direction, images)

    def both_cores(own_ref, got_ref, *refs):
        out_ref = refs[levels]
        out_ref[...] = own_ref[...] + got_ref[...]

    vmem, anywhere = pl.BlockSpec(memory_space=pltpu.VMEM), pl.BlockSpec(memory_space=pl.ANY)
    delta, *images = pl.pallas_call(
        both_cores,
        out_shape=[jax.ShapeDtypeStruct(*scalar)] + [jax.ShapeDtypeStruct((rows, outs), F32) for rows in piece_rows],
        in_specs=[vmem, vmem] + [anywhere] * levels,
        out_specs=[vmem] + [anywhere] * levels,
        input_output_aliases={2 + index: 1 + index for index in range(levels)},
        compiler_params=pltpu.CompilerParams(vmem_limit_bytes=LIMIT),
    )(part, over_group(1, part), *images)
    other_images = [over_group(1, image) for image in images]
    other_residual = over_group(1, residual)
    got = {step: over_row(step, delta) for step in row_steps}
    deltas = [delta] + [got[step] for step in range(1, n_row)]

    def finish(*refs):
        delta_refs, refs = refs[:n_row], refs[n_row:]
        image_refs, refs = refs[:levels], refs[levels:]
        other_image_refs, refs = refs[:levels], refs[levels:]
        gamma_ref, sq_ref, ridge_ref, r_ref, other_r_ref, dir_ref, w_ref, w_out, r_out = refs
        image_sq = tree_sum([ref[0:1, :] for ref in delta_refs])
        alpha = gamma_ref[0:1, :] / (image_sq + ridge_ref[...] * sq_ref[0:1, :])
        w_out[...] = w_ref[...] + alpha * dir_ref[...]
        for core_step, old_ref, refs in ((0, r_ref, image_refs), (1, other_r_ref, other_image_refs)):
            for ref, start, rows in zip(refs, piece_starts, piece_rows):
                place = pl.ds(pl.multiple_of(token_place(core_step) + start, 64), rows)
                r_out[place, :] = old_ref[pl.ds(start, rows), :] - alpha * ref[...]

    weights, residual = call(
        finish,
        [feature_rows, ((tokens, outs), F32)],
        [*deltas, *images, *other_images, gamma, dir_sq, ridge, residual, other_residual, direction, *weights],
    )
    return weights, residual


def solution(mesh):
    placed = (P("row", "group"), P("row", None), P())
    return jax.shard_map(
        shards,
        mesh=mesh,
        in_specs=placed,
        out_specs=(P(("group", "row"), None), P("row", None)),
        check_vma=False,
    )
```

```python
import functools

import jax
import jax.numpy as jnp
from jax import lax
from jax.experimental import pallas as pl
from jax.experimental.pallas import tpu as pltpu
from jax.sharding import PartitionSpec as P

ITERS = 3
PAD = 16
F32 = jnp.float32
BF16 = jnp.bfloat16
F16 = jnp.float16
ROW_WIRE = (F16, F16, BF16)
CORE_WIRE = (F32, F32, F32)
CHIP_WIRE = ((BF16, BF16), (BF16, BF16), (BF16, BF16))
FIRST_PIECE = 9
ROW_ORDER = 1
LIMIT = 24 * 1024 * 1024


def tree_sum(terms):
    terms = list(terms)
    while len(terms) > 1:
        terms = [terms[i] + terms[i + 1] for i in range(0, len(terms), 2)]
    return terms[0]


def put_rows(ref, *values):
    rows = ref.shape[0] - PAD
    parts = []
    for value in values:
        high = value.astype(BF16).astype(F32)
        middle = (value - high).astype(BF16).astype(F32)
        parts += [high, middle, value - high - middle]
    shape = (PAD, ref.shape[1])
    index = lax.broadcasted_iota(jnp.int32, shape, 0)
    block = jnp.zeros(shape, F32)
    for place, part in enumerate(parts):
        block = jnp.where(index == place, jnp.broadcast_to(part, shape), block)
    ref[pl.ds(rows, PAD), :] = block.astype(ref.dtype)


def get_row(ref, which=0):
    rows = ref.shape[0] - PAD
    tail = ref[pl.ds(rows, PAD), :].astype(F32)
    at = 3 * which
    return tail[at : at + 1] + tail[at + 1 : at + 2] + tail[at + 2 : at + 3]


def exponent_of(value):
    return jnp.clip(jnp.floor(jnp.log2(jnp.maximum(value, 1e-36))), -119.0, 119.0)


def put_scaled(ref, exponent, value):
    rows = ref.shape[0] - PAD
    own = exponent_of(value)
    scaled = value * jnp.exp2(-own)
    high = scaled.astype(BF16).astype(F32)
    middle = (scaled - high).astype(BF16).astype(F32)
    parts = [exponent, own, high, 256.0 * middle, 65536.0 * (scaled - high - middle)]
    shape = (PAD, ref.shape[1])
    index = lax.broadcasted_iota(jnp.int32, shape, 0)
    block = jnp.zeros(shape, F32)
    for place, part in enumerate(parts):
        block = jnp.where(index == place, jnp.broadcast_to(part, shape), block)
    ref[pl.ds(rows, PAD), :] = block


def get_scaled(ref):
    rows = ref.shape[0] - PAD
    tail = ref[pl.ds(rows, PAD), :]
    value = tail[2:3] + tail[3:4] * (1.0 / 256.0) + tail[4:5] * (1.0 / 65536.0)
    return jnp.exp2(tail[0:1]), value * jnp.exp2(tail[1:2])


def body_of(ref):
    return ref[pl.ds(0, ref.shape[0] - PAD), :]


def column_sum(values):
    return jnp.sum(values, axis=0, keepdims=True)


def spread(ref, value):
    ref[...] = jnp.broadcast_to(value, ref.shape)


def call(kernel, outs, operands, scratch=()):
    vmem = pl.BlockSpec(memory_space=pltpu.VMEM)
    return pl.pallas_call(
        kernel,
        out_shape=[jax.ShapeDtypeStruct(shape, dtype) for shape, dtype in outs],
        in_specs=[vmem] * len(operands),
        out_specs=[vmem] * len(outs),
        scratch_shapes=scratch,
        compiler_params=pltpu.CompilerParams(vmem_limit_bytes=LIMIT),
    )(*operands)


def shards(states, targets, ridge):
    n_row = lax.axis_size("row")
    n_group = lax.axis_size("group")
    levels = (n_group // 2).bit_length() - 1
    tokens, feats = states.shape
    outs = targets.shape[1]
    feat_share = feats // n_row
    half = tokens // 2
    piece_rows = [half // levels] * levels
    if levels == 2:
        piece_rows = [half * FIRST_PIECE // 16, half - half * FIRST_PIECE // 16]
    piece_starts = [sum(piece_rows[:index]) for index in range(levels)]
    row_steps = list(range(1, n_row))[::ROW_ORDER]
    block = 256
    ridge = ridge.reshape(1, outs)
    scalar = ((8, outs), F32)
    feature_rows = ((feat_share, outs), F32)
    token_rows = ((half, outs), F32)

    def over_row(step, value):
        return lax.ppermute(value, "row", [(i, i ^ step) for i in range(n_row)])

    def over_group(step, value):
        return lax.ppermute(value, "group", [(i, i ^ step) for i in range(n_group)])

    def row_place(step):
        return pl.multiple_of((lax.axis_index("row") ^ step) * feat_share, feat_share)

    def token_place(core_step):
        core = (lax.axis_index("group") % 2) ^ core_step
        return pl.multiple_of(core * half, half)

    def cut(wire, prod, delta, own_ref, msg_refs):
        own_ref[...] = prod[pl.ds(row_place(0), feat_share), :]
        if wire == F16:
            exponent = exponent_of(jnp.max(jnp.abs(prod[...]), axis=0, keepdims=True))
            factor = jnp.exp2(-exponent)
        for step, ref in zip(row_steps, msg_refs):
            part = prod[pl.ds(row_place(step), feat_share), :]
            if wire == F16:
                ref[pl.ds(0, feat_share), :] = part * factor
                put_scaled(ref, exponent, delta)
            else:
                ref[pl.ds(0, feat_share), :] = part.astype(wire)
                put_rows(ref, delta)

    def put_block(wire, ref, part, delta):
        if wire == F16:
            exponent = exponent_of(jnp.max(jnp.abs(part), axis=0, keepdims=True))
            ref[pl.ds(0, feat_share), :] = part * jnp.exp2(-exponent)
            put_scaled(ref, exponent, delta)
        else:
            ref[pl.ds(0, feat_share), :] = part.astype(wire)
            put_rows(ref, delta)

    by_block = feat_share % 128 == 0

    def columns(step):
        return pl.ds(row_place(step), feat_share)

    def cut_shapes(wire):
        return [((feat_share + PAD, outs), F32 if wire == F16 else wire)] * (n_row - 1)

    def scattered(wire, sends):
        got = {step: over_row(step, send.astype(wire)) for step, send in zip(row_steps, sends)}
        got = [got[step] for step in range(1, n_row)]
        return [send.astype(F32) if wire == F16 else send for send in got]

    def backward_first(wire):
        def split(t_ref, turned_ref, r_out):
            for start in range(0, tokens, block):
                whole = t_ref[start : start + block, :]
                high = whole.astype(BF16)
                turned_ref[0:outs, start : start + block] = high.T
                turned_ref[outs : 2 * outs, start : start + block] = (whole - high.astype(F32)).astype(BF16).T
            r_out[...] = t_ref[pl.ds(token_place(0), half), :]

        def product(a_ref, turned_ref, own_ref, *refs):
            *msg_refs, prod = refs
            for start in range(0, feats, block):
                cols = slice(start, start + block)
                part = jnp.dot(turned_ref[...], a_ref[:, cols], preferred_element_type=F32)
                prod[cols, :] = (part[0:outs] + part[outs : 2 * outs]).T
            cut(wire, prod, jnp.zeros((1, outs), F32), own_ref, msg_refs)

        def block_product(a_ref, turned_ref, step):
            part = jnp.dot(turned_ref[...], a_ref[:, columns(step)], preferred_element_type=F32)
            return (part[0:outs] + part[outs : 2 * outs]).T

        def messages(a_ref, turned_ref, *msg_refs):
            for step, ref in zip(row_steps, msg_refs):
                put_block(wire, ref, block_product(a_ref, turned_ref, step), jnp.zeros((1, outs), F32))

        def own_block(a_ref, turned_ref, own_ref):
            own_ref[...] = block_product(a_ref, turned_ref, 0)

        turned, residual = call(split, [((2 * outs, tokens), BF16), token_rows], [targets])
        if by_block:
            got = scattered(wire, call(messages, cut_shapes(wire), [states, turned]))
            (own,) = call(own_block, [feature_rows], [states, turned])
            return residual, own, got
        own, *sends = call(
            product,
            [feature_rows] + cut_shapes(wire),
            [states, turned],
            [pltpu.VMEM((feats, outs), F32)],
        )
        return residual, own, scattered(wire, sends)

    def backward(wire, mine, theirs):
        def half_product(a_ref, refs, core_step, cols):
            total = None
            for ref, start, rows in zip(refs, piece_starts, piece_rows):
                place = pl.ds(pl.multiple_of(token_place(core_step) + start, 64), rows)
                part = jnp.dot(ref[pl.ds(0, rows), :].T, a_ref[place, cols], preferred_element_type=F32)
                total = part if total is None else total + part
            return total

        def first_half(a_ref, *refs):
            *mine_refs, part_ref = refs
            for start in range(0, feats, block):
                cols = slice(start, start + block)
                part_ref[:, cols] = half_product(a_ref, mine_refs, 0, cols)

        def second_half(a_ref, *refs):
            mine_ref, theirs_refs = refs[0], refs[1 : levels + 1]
            part_ref, own_ref, delta_ref, *msg_refs, prod = refs[levels + 1 :]
            delta = get_row(mine_ref) + get_row(theirs_refs[-1])
            spread(delta_ref, delta)
            for start in range(0, feats, block):
                cols = slice(start, start + block)
                prod[cols, :] = (part_ref[:, cols] + half_product(a_ref, theirs_refs, 1, cols)).T
            cut(wire, prod, delta, own_ref, msg_refs)

        def block_product(a_ref, part_ref, refs, step):
            return (part_ref[:, columns(step)] + half_product(a_ref, refs, 1, columns(step))).T

        def messages(a_ref, *refs):
            mine_ref, theirs_refs, part_ref = refs[0], refs[1 : levels + 1], refs[levels + 1]
            delta_ref, *msg_refs = refs[levels + 2 :]
            delta = get_row(mine_ref) + get_row(theirs_refs[-1])
            spread(delta_ref, delta)
            for step, ref in zip(row_steps, msg_refs):
                put_block(wire, ref, block_product(a_ref, part_ref, theirs_refs, step), delta)

        def own_block(a_ref, *refs):
            *theirs_refs, part_ref, own_ref = refs
            own_ref[...] = block_product(a_ref, part_ref, theirs_refs, 0)

        (part,) = call(first_half, [((outs, feats), F32)], [states, *mine])
        if by_block:
            delta, *sends = call(
                messages, [scalar] + cut_shapes(wire), [states, mine[-1], *theirs, part]
            )
            got = scattered(wire, sends)
            (own,) = call(own_block, [feature_rows], [states, *theirs, part])
            return own, delta, got
        own, delta, *sends = call(
            second_half,
            [feature_rows, scalar] + cut_shapes(wire),
            [states, mine[-1], *theirs, part],
            [pltpu.VMEM((feats, outs), F32)],
        )
        return own, delta, scattered(wire, sends)

    def begin(own, got):
        def kernel(own_ref, *refs):
            ins, (grad_ref, msg_ref) = refs[: n_row - 1], refs[n_row - 1 :]
            grad = own_ref[...]
            for ref in ins:
                grad = grad + get_scaled(ref)[0] * body_of(ref)
            grad_ref[...] = grad
            msg_ref[pl.ds(0, feat_share), :] = grad.astype(BF16)
            put_rows(msg_ref, column_sum(grad * grad), jnp.zeros((1, outs), F32))

        return call(kernel, [feature_rows, ((feat_share + PAD, outs), BF16)], [own] + got)

    def advance(wire, own, delta, got, gamma, dir_sq, grad, direction, images, weights, residual):
        def kernel(own_ref, delta_ref, *refs):
            ins = refs[: n_row - 1]
            gamma_ref, sq_ref, grad_ref, dir_ref, r_ref, ridge_ref = refs[n_row - 1 : n_row + 5]
            image_refs = refs[n_row + 5 : n_row + 5 + levels]
            *w_ref, w_out, r_out, grad_out, msg_ref = refs[n_row + 5 + levels :]
            if wire == F16:
                tails = [get_scaled(ref) for ref in ins]
            else:
                tails = [(1.0, get_row(ref)) for ref in ins]
            image_sq = tree_sum([delta_ref[0:1, :]] + [value for _, value in tails])
            alpha = gamma_ref[0:1, :] / (image_sq + ridge_ref[...] * sq_ref[0:1, :])
            prod = own_ref[...]
            for ref, (scale, _) in zip(ins, tails):
                prod = prod + scale * body_of(ref).astype(F32)
            old_dir = dir_ref[...]
            new = grad_ref[...] - alpha * (prod + ridge_ref[...] * old_dir)
            msg_ref[pl.ds(0, feat_share), :] = new.astype(BF16)
            put_rows(msg_ref, column_sum(new * new), column_sum(new * old_dir))
            grad_out[...] = new
            step_taken = alpha * old_dir
            w_out[...] = w_ref[0][...] + step_taken if w_ref else step_taken
            for ref, start, rows in zip(image_refs, piece_starts, piece_rows):
                place = pl.ds(start, rows)
                r_out[place, :] = r_ref[place, :] - alpha * ref[...]

        return call(
            kernel,
            [feature_rows, token_rows, feature_rows, ((feat_share + PAD, outs), BF16)],
            [own, delta, *got, gamma, dir_sq, grad, direction, residual, ridge, *images, *weights],
        )

    def forward(wire, msg):
        got = {step: over_row(step, msg) for step in row_steps}
        blocks = [msg] + [got[step] for step in range(1, n_row)]

        def product(a_ref, vec, core_step, index, ref):
            start, rows = piece_starts[index], piece_rows[index]
            place = pl.ds(pl.multiple_of(token_place(core_step) + start, 64), rows)
            part = jnp.dot(a_ref[place, :], vec[...], preferred_element_type=F32)
            ref[pl.ds(0, rows), :] = part.astype(ref.dtype)

        def first_piece(a_ref, *refs):
            ins = refs[:n_row]
            peer_ref, gamma_ref, cross_ref, vec = refs[n_row:]
            for step, ref in enumerate(ins):
                vec[pl.ds(row_place(step), feat_share), :] = body_of(ref)
            gamma = tree_sum([get_row(ref, 0) for ref in ins])
            cross = tree_sum([get_row(ref, 1) for ref in ins])
            spread(gamma_ref, gamma)
            spread(cross_ref, cross)
            product(a_ref, vec, 1, 0, peer_ref)
            put_rows(peer_ref, gamma, cross)

        def later_piece(index, a_ref, vec, peer_ref):
            product(a_ref, vec, 1, index, peer_ref)

        def own_pieces(a_ref, vec, *refs):
            for index, ref in enumerate(refs):
                product(a_ref, vec, 0, index, ref)

        peer, gamma, cross, vec = call(
            first_piece,
            [pieces(wire)[0], scalar, scalar, ((feats, outs), BF16)],
            [states] + blocks,
        )
        got = [over_group(1, peer)]
        for index in range(1, levels):
            (peer,) = call(functools.partial(later_piece, index), [pieces(wire)[index]], [states, vec])
            got.append(over_group(1, peer))
        own = call(own_pieces, [((rows, outs), F32) for rows in piece_rows], [states, vec])
        return own, gamma, cross, got

    def pieces(wire):
        return [((rows + (0 if index else PAD), outs), wire) for index, rows in enumerate(piece_rows)]

    def swapped(step, sends):
        return [
            over_group(2 << ((index + step) % levels), send) for index, send in enumerate(sends)
        ]

    def join_cores(wire, own, gamma, cross, got):
        def kernel(own_ref, got_ref, *refs):
            *scalars, out_ref = refs
            place = pl.ds(0, own_ref.shape[0])
            out_ref[place, :] = (own_ref[...] + got_ref[place, :].astype(F32)).astype(wire)
            if scalars:
                put_rows(out_ref, *[ref[0:1, :] + get_row(got_ref, k) for k, ref in enumerate(scalars)])

        return [
            call(kernel, [shape], [own[index], got[index]] + ([] if index else [gamma, cross]))[0]
            for index, shape in enumerate(pieces(wire))
        ]

    def join_chips(wire, sent, got):
        def kernel(has_scalars, rows, own_ref, got_ref, out_ref):
            place = pl.ds(0, rows)
            both = own_ref[place, :].astype(F32) + got_ref[place, :].astype(F32)
            out_ref[place, :] = both.astype(wire)
            if has_scalars:
                put_rows(out_ref, *[get_row(own_ref, k) + get_row(got_ref, k) for k in range(2)])

        return [
            call(functools.partial(kernel, index == 0, piece_rows[index]), [shape], [sent[index], got[index]])[0]
            for index, shape in enumerate(pieces(wire))
        ]

    def image_of(last, sent, got, grad, before):
        def first_piece(own_ref, got_ref, grad_ref, *refs):
            old, (gamma_out, beta_out, sq_out, dir_out, *outputs) = refs[:-6 - more], refs[-6 - more :]
            gamma, cross = [get_row(own_ref, k) + get_row(got_ref, k) for k in range(2)]
            spread(gamma_out, gamma)
            direction = grad_ref[...]
            dir_sq = gamma
            beta = None
            if before:
                old_gamma, old_sq, old_dir = old[:3]
                beta = gamma / old_gamma[0:1, :]
                direction = direction + beta * old_dir[...]
                dir_sq = gamma + beta * (2.0 * cross + beta * old_sq[0:1, :])
                spread(beta_out, beta)
            else:
                spread(beta_out, gamma)
            dir_out[...] = direction
            spread(sq_out, dir_sq)
            part = piece_image(0, own_ref, got_ref, beta, old[3:], outputs)
            spread(outputs[-1], part)

        def later_piece(index, own_ref, got_ref, part_ref, beta_ref, *refs):
            count = len(shapes(index))
            old, outputs = refs[:-count], refs[-count:]
            part = part_ref[0:1, :] + piece_image(index, own_ref, got_ref, beta_ref[0:1, :], old, outputs)
            if not last and index + 1 == levels:
                put_rows(outputs[1], part)
            else:
                spread(outputs[-1], part)

        def piece_image(index, own_ref, got_ref, beta, old, outputs):
            place = pl.ds(0, piece_rows[index])
            image = own_ref[place, :].astype(F32) + got_ref[place, :].astype(F32)
            if before:
                image = image + beta * old[0][...]
            outputs[0][...] = image
            if not last:
                outputs[1][place, :] = image.astype(BF16)
            return column_sum(image * image)

        more = 0 if last else 1

        def shapes(index):
            rows = piece_rows[index]
            tail = PAD if index + 1 == levels else 0
            shape = [((rows, outs), F32)] + [((rows + tail, outs), BF16)] * more
            return shape + [scalar] if last or index + 1 < levels else shape

        gamma, beta, dir_sq, direction, image, *msg, part = call(
            first_piece,
            [scalar, scalar, scalar, feature_rows] + shapes(0),
            [sent[0], got[0], grad] + list(before[:3]) + list(before[3][:1] if before else ()),
        )
        images, msgs = [image], msg
        for index in range(1, levels):
            image, *msg = call(
                functools.partial(later_piece, index),
                shapes(index),
                [sent[index], got[index], part, beta] + list(before[3][index : index + 1] if before else ()),
            )
            if last or index + 1 < levels:
                *msg, part = msg
            images.append(image)
            msgs += msg
        return gamma, dir_sq, direction, images, msgs, part

    weights = ()
    residual, own, got = backward_first(ROW_WIRE[0])
    grad, msg = begin(own, got)
    before = ()
    for step in range(ITERS):
        own, gamma, cross, got = forward(CORE_WIRE[step], msg)
        sent = join_cores(CHIP_WIRE[step][0], own, gamma, cross, got)
        got = swapped(0, sent)
        for level in range(1, levels):
            sent = join_chips(CHIP_WIRE[step][1], sent, got)
            got = swapped(level, sent)
        last = step + 1 == ITERS
        gamma, dir_sq, direction, images, msgs, part = image_of(last, sent, got, grad, before)
        if not last:
            own, delta, got = backward(
                ROW_WIRE[step + 1], msgs, [over_group(1, msg) for msg in msgs]
            )
            new, residual, grad, msg = advance(
                ROW_WIRE[step + 1], own, delta, got, gamma, dir_sq, grad, direction, images, weights, residual
            )
            weights = (new,)
            before = (gamma, dir_sq, direction, images)

    def both_cores(own_ref, got_ref, *refs):
        out_ref = refs[levels - 1]
        out_ref[...] = own_ref[...] + got_ref[...]

    vmem, anywhere = pl.BlockSpec(memory_space=pltpu.VMEM), pl.BlockSpec(memory_space=pl.ANY)
    delta, *later = pl.pallas_call(
        both_cores,
        out_shape=[jax.ShapeDtypeStruct(*scalar)] + [jax.ShapeDtypeStruct((rows, outs), F32) for rows in piece_rows[1:]],
        in_specs=[vmem, vmem] + [anywhere] * (levels - 1),
        out_specs=[vmem] + [anywhere] * (levels - 1),
        input_output_aliases={2 + index: 1 + index for index in range(levels - 1)},
        compiler_params=pltpu.CompilerParams(vmem_limit_bytes=LIMIT),
    )(part, over_group(1, part), *images[1:])
    images = [images[0], *later]
    other_images = [over_group(1, image) for image in images]
    other_residual = over_group(1, residual)
    got = {step: over_row(step, delta) for step in row_steps}
    deltas = [delta] + [got[step] for step in range(1, n_row)]

    def finish(*refs):
        delta_refs, refs = refs[:n_row], refs[n_row:]
        image_refs, refs = refs[:levels], refs[levels:]
        other_image_refs, refs = refs[:levels], refs[levels:]
        gamma_ref, sq_ref, ridge_ref, r_ref, other_r_ref, dir_ref, w_ref, w_out, r_out = refs
        image_sq = tree_sum([ref[0:1, :] for ref in delta_refs])
        alpha = gamma_ref[0:1, :] / (image_sq + ridge_ref[...] * sq_ref[0:1, :])
        w_out[...] = w_ref[...] + alpha * dir_ref[...]
        for core_step, old_ref, refs in ((0, r_ref, image_refs), (1, other_r_ref, other_image_refs)):
            for ref, start, rows in zip(refs, piece_starts, piece_rows):
                place = pl.ds(pl.multiple_of(token_place(core_step) + start, 64), rows)
                r_out[place, :] = old_ref[pl.ds(start, rows), :] - alpha * ref[...]

    weights, residual = call(
        finish,
        [feature_rows, ((tokens, outs), F32)],
        [*deltas, *images, *other_images, gamma, dir_sq, ridge, residual, other_residual, direction, *weights],
    )
    return weights, residual


def solution(mesh):
    placed = (P("row", "group"), P("row", None), P())
    return jax.shard_map(
        shards,
        mesh=mesh,
        in_specs=placed,
        out_specs=(P(("group", "row"), None), P("row", None)),
        check_vma=False,
    )
```

```python
import functools

import jax
import jax.numpy as jnp
from jax import lax
from jax.experimental import pallas as pl
from jax.experimental.pallas import tpu as pltpu
from jax.sharding import PartitionSpec as P

ITERS = 3
PAD = 16
TWO_PARTS = (1,)
F32 = jnp.float32
BF16 = jnp.bfloat16
F16 = jnp.float16
ROW_WIRE = (F16, F16, BF16)
CORE_WIRE = (F32, F32, F32)
CHIP_WIRE = ((BF16, BF16), (BF16, BF16), (BF16, BF16))
FIRST_PIECE = 9
ROW_ORDER = 1
LIMIT = 24 * 1024 * 1024


def tree_sum(terms):
    terms = list(terms)
    while len(terms) > 1:
        terms = [terms[i] + terms[i + 1] for i in range(0, len(terms), 2)]
    return terms[0]


def put_rows(ref, *values):
    rows = ref.shape[0] - PAD
    parts = []
    for value in values:
        high = value.astype(BF16).astype(F32)
        middle = (value - high).astype(BF16).astype(F32)
        parts += [high, middle, value - high - middle]
    shape = (PAD, ref.shape[1])
    index = lax.broadcasted_iota(jnp.int32, shape, 0)
    block = jnp.zeros(shape, F32)
    for place, part in enumerate(parts):
        block = jnp.where(index == place, jnp.broadcast_to(part, shape), block)
    ref[pl.ds(rows, PAD), :] = block.astype(ref.dtype)


def get_row(ref, which=0):
    rows = ref.shape[0] - PAD
    tail = ref[pl.ds(rows, PAD), :].astype(F32)
    at = 3 * which
    return tail[at : at + 1] + tail[at + 1 : at + 2] + tail[at + 2 : at + 3]


def exponent_of(value):
    return jnp.clip(jnp.floor(jnp.log2(jnp.maximum(value, 1e-36))), -119.0, 119.0)


def put_scaled(ref, exponent, value):
    rows = ref.shape[0] - PAD
    own = exponent_of(value)
    scaled = value * jnp.exp2(-own)
    high = scaled.astype(BF16).astype(F32)
    middle = (scaled - high).astype(BF16).astype(F32)
    parts = [exponent, own, high, 256.0 * middle, 65536.0 * (scaled - high - middle)]
    shape = (PAD, ref.shape[1])
    index = lax.broadcasted_iota(jnp.int32, shape, 0)
    block = jnp.zeros(shape, F32)
    for place, part in enumerate(parts):
        block = jnp.where(index == place, jnp.broadcast_to(part, shape), block)
    ref[pl.ds(rows, PAD), :] = block


def get_scaled(ref):
    rows = ref.shape[0] - PAD
    tail = ref[pl.ds(rows, PAD), :]
    value = tail[2:3] + tail[3:4] * (1.0 / 256.0) + tail[4:5] * (1.0 / 65536.0)
    return jnp.exp2(tail[0:1]), value * jnp.exp2(tail[1:2])


def body_of(ref):
    return ref[pl.ds(0, ref.shape[0] - PAD), :]


def column_sum(values):
    return jnp.sum(values, axis=0, keepdims=True)


def spread(ref, value):
    ref[...] = jnp.broadcast_to(value, ref.shape)


def call(kernel, outs, operands, scratch=()):
    vmem = pl.BlockSpec(memory_space=pltpu.VMEM)
    return pl.pallas_call(
        kernel,
        out_shape=[jax.ShapeDtypeStruct(shape, dtype) for shape, dtype in outs],
        in_specs=[vmem] * len(operands),
        out_specs=[vmem] * len(outs),
        scratch_shapes=scratch,
        compiler_params=pltpu.CompilerParams(vmem_limit_bytes=LIMIT),
    )(*operands)


def shards(states, targets, ridge):
    n_row = lax.axis_size("row")
    n_group = lax.axis_size("group")
    levels = (n_group // 2).bit_length() - 1
    tokens, feats = states.shape
    outs = targets.shape[1]
    feat_share = feats // n_row
    half = tokens // 2
    piece_rows = [half // levels] * levels
    if levels == 2:
        piece_rows = [half * FIRST_PIECE // 16, half - half * FIRST_PIECE // 16]
    piece_starts = [sum(piece_rows[:index]) for index in range(levels)]
    row_steps = list(range(1, n_row))[::ROW_ORDER]
    block = 256
    ridge = ridge.reshape(1, outs)
    scalar = ((8, outs), F32)
    feature_rows = ((feat_share, outs), F32)
    token_rows = ((half, outs), F32)

    def over_row(step, value):
        return lax.ppermute(value, "row", [(i, i ^ step) for i in range(n_row)])

    def over_group(step, value):
        return lax.ppermute(value, "group", [(i, i ^ step) for i in range(n_group)])

    def row_place(step):
        return pl.multiple_of((lax.axis_index("row") ^ step) * feat_share, feat_share)

    def token_place(core_step):
        core = (lax.axis_index("group") % 2) ^ core_step
        return pl.multiple_of(core * half, half)

    def cut(wire, prod, delta, own_ref, msg_refs):
        own_ref[...] = prod[pl.ds(row_place(0), feat_share), :]
        if wire == F16:
            exponent = exponent_of(jnp.max(jnp.abs(prod[...]), axis=0, keepdims=True))
            factor = jnp.exp2(-exponent)
        for step, ref in zip(row_steps, msg_refs):
            part = prod[pl.ds(row_place(step), feat_share), :]
            if wire == F16:
                ref[pl.ds(0, feat_share), :] = part * factor
                put_scaled(ref, exponent, delta)
            else:
                ref[pl.ds(0, feat_share), :] = part.astype(wire)
                put_rows(ref, delta)

    def put_block(wire, ref, part, delta):
        if wire == F16:
            exponent = exponent_of(jnp.max(jnp.abs(part), axis=0, keepdims=True))
            ref[pl.ds(0, feat_share), :] = part * jnp.exp2(-exponent)
            put_scaled(ref, exponent, delta)
        else:
            ref[pl.ds(0, feat_share), :] = part.astype(wire)
            put_rows(ref, delta)

    by_block = feat_share % 128 == 0

    def columns(step):
        return pl.ds(row_place(step), feat_share)

    def cut_shapes(wire):
        return [((feat_share + PAD, outs), F32 if wire == F16 else wire)] * (n_row - 1)

    def scattered(wire, sends):
        got = {step: over_row(step, send.astype(wire)) for step, send in zip(row_steps, sends)}
        got = [got[step] for step in range(1, n_row)]
        return [send.astype(F32) if wire == F16 else send for send in got]

    def backward_first(wire):
        def split(t_ref, turned_ref, r_out):
            for start in range(0, tokens, block):
                whole = t_ref[start : start + block, :]
                high = whole.astype(BF16)
                turned_ref[0:outs, start : start + block] = high.T
                turned_ref[outs : 2 * outs, start : start + block] = (whole - high.astype(F32)).astype(BF16).T
            r_out[...] = t_ref[pl.ds(token_place(0), half), :]

        def product(a_ref, turned_ref, own_ref, *refs):
            *msg_refs, prod = refs
            for start in range(0, feats, block):
                cols = slice(start, start + block)
                part = jnp.dot(turned_ref[...], a_ref[:, cols], preferred_element_type=F32)
                prod[cols, :] = (part[0:outs] + part[outs : 2 * outs]).T
            cut(wire, prod, jnp.zeros((1, outs), F32), own_ref, msg_refs)

        def block_product(a_ref, turned_ref, step):
            part = jnp.dot(turned_ref[...], a_ref[:, columns(step)], preferred_element_type=F32)
            return (part[0:outs] + part[outs : 2 * outs]).T

        def messages(a_ref, turned_ref, *msg_refs):
            for step, ref in zip(row_steps, msg_refs):
                put_block(wire, ref, block_product(a_ref, turned_ref, step), jnp.zeros((1, outs), F32))

        def own_block(a_ref, turned_ref, own_ref):
            own_ref[...] = block_product(a_ref, turned_ref, 0)

        turned, residual = call(split, [((2 * outs, tokens), BF16), token_rows], [targets])
        if by_block:
            got = scattered(wire, call(messages, cut_shapes(wire), [states, turned]))
            (own,) = call(own_block, [feature_rows], [states, turned])
            return residual, own, got
        own, *sends = call(
            product,
            [feature_rows] + cut_shapes(wire),
            [states, turned],
            [pltpu.VMEM((feats, outs), F32)],
        )
        return residual, own, scattered(wire, sends)

    def backward(wire, mine, theirs):
        def half_product(a_ref, refs, core_step, cols):
            total = None
            for ref, start, rows in zip(refs, piece_starts, piece_rows):
                place = pl.ds(pl.multiple_of(token_place(core_step) + start, 64), rows)
                part = jnp.dot(ref[pl.ds(0, rows), :].T, a_ref[place, cols], preferred_element_type=F32)
                total = part if total is None else total + part
            return total

        def first_half(a_ref, *refs):
            *mine_refs, part_ref = refs
            for start in range(0, feats, block):
                cols = slice(start, start + block)
                part_ref[:, cols] = half_product(a_ref, mine_refs, 0, cols)

        def second_half(a_ref, *refs):
            mine_ref, theirs_refs = refs[0], refs[1 : levels + 1]
            part_ref, own_ref, delta_ref, *msg_refs, prod = refs[levels + 1 :]
            delta = get_row(mine_ref) + get_row(theirs_refs[-1])
            spread(delta_ref, delta)
            for start in range(0, feats, block):
                cols = slice(start, start + block)
                prod[cols, :] = (part_ref[:, cols] + half_product(a_ref, theirs_refs, 1, cols)).T
            cut(wire, prod, delta, own_ref, msg_refs)

        def block_product(a_ref, part_ref, refs, step):
            return (part_ref[:, columns(step)] + half_product(a_ref, refs, 1, columns(step))).T

        def messages(a_ref, *refs):
            mine_ref, theirs_refs, part_ref = refs[0], refs[1 : levels + 1], refs[levels + 1]
            delta_ref, *msg_refs = refs[levels + 2 :]
            delta = get_row(mine_ref) + get_row(theirs_refs[-1])
            spread(delta_ref, delta)
            for step, ref in zip(row_steps, msg_refs):
                put_block(wire, ref, block_product(a_ref, part_ref, theirs_refs, step), delta)

        def own_block(a_ref, *refs):
            *theirs_refs, part_ref, own_ref = refs
            own_ref[...] = block_product(a_ref, part_ref, theirs_refs, 0)

        (part,) = call(first_half, [((outs, feats), F32)], [states, *mine])
        if by_block:
            delta, *sends = call(
                messages, [scalar] + cut_shapes(wire), [states, mine[-1], *theirs, part]
            )
            got = scattered(wire, sends)
            (own,) = call(own_block, [feature_rows], [states, *theirs, part])
            return own, delta, got
        own, delta, *sends = call(
            second_half,
            [feature_rows, scalar] + cut_shapes(wire),
            [states, mine[-1], *theirs, part],
            [pltpu.VMEM((feats, outs), F32)],
        )
        return own, delta, scattered(wire, sends)

    def begin(own, got):
        def kernel(own_ref, *refs):
            ins, (grad_ref, msg_ref) = refs[: n_row - 1], refs[n_row - 1 :]
            grad = own_ref[...]
            for ref in ins:
                grad = grad + get_scaled(ref)[0] * body_of(ref)
            grad_ref[...] = grad
            msg_ref[pl.ds(0, feat_share), :] = grad.astype(BF16)
            put_rows(msg_ref, column_sum(grad * grad), jnp.zeros((1, outs), F32))

        return call(kernel, [feature_rows, ((feat_share + PAD, outs), BF16)], [own] + got)

    def advance(wire, own, delta, got, gamma, dir_sq, grad, direction, images, weights, residual):
        def kernel(own_ref, delta_ref, *refs):
            ins = refs[: n_row - 1]
            gamma_ref, sq_ref, grad_ref, dir_ref, r_ref, ridge_ref = refs[n_row - 1 : n_row + 5]
            image_refs = refs[n_row + 5 : n_row + 5 + levels]
            *w_ref, w_out, r_out, grad_out, msg_ref = refs[n_row + 5 + levels :]
            if wire == F16:
                tails = [get_scaled(ref) for ref in ins]
            else:
                tails = [(1.0, get_row(ref)) for ref in ins]
            image_sq = tree_sum([delta_ref[0:1, :]] + [value for _, value in tails])
            alpha = gamma_ref[0:1, :] / (image_sq + ridge_ref[...] * sq_ref[0:1, :])
            prod = own_ref[...]
            for ref, (scale, _) in zip(ins, tails):
                prod = prod + scale * body_of(ref).astype(F32)
            old_dir = dir_ref[...]
            new = grad_ref[...] - alpha * (prod + ridge_ref[...] * old_dir)
            msg_ref[pl.ds(0, feat_share), :] = new.astype(BF16)
            put_rows(msg_ref, column_sum(new * new), column_sum(new * old_dir))
            grad_out[...] = new
            step_taken = alpha * old_dir
            w_out[...] = w_ref[0][...] + step_taken if w_ref else step_taken
            for ref, start, rows in zip(image_refs, piece_starts, piece_rows):
                place = pl.ds(start, rows)
                r_out[place, :] = r_ref[place, :] - alpha * ref[...]

        return call(
            kernel,
            [feature_rows, token_rows, feature_rows, ((feat_share + PAD, outs), BF16)],
            [own, delta, *got, gamma, dir_sq, grad, direction, residual, ridge, *images, *weights],
        )

    def forward(wire, in_two, msg):
        got = {step: over_row(step, msg) for step in row_steps}
        blocks = [msg] + [got[step] for step in range(1, n_row)]

        def product(a_ref, vec, core_step, index, ref):
            start, rows = piece_starts[index], piece_rows[index]
            place = pl.ds(pl.multiple_of(token_place(core_step) + start, 64), rows)
            part = jnp.dot(a_ref[place, :], vec[...], preferred_element_type=F32)
            ref[pl.ds(0, rows), :] = part.astype(ref.dtype)

        def first_piece(a_ref, *refs):
            ins = refs[:n_row]
            peer_ref, gamma_ref, cross_ref, vec = refs[n_row:]
            for step, ref in enumerate(ins):
                vec[pl.ds(row_place(step), feat_share), :] = body_of(ref)
            gamma = tree_sum([get_row(ref, 0) for ref in ins])
            cross = tree_sum([get_row(ref, 1) for ref in ins])
            spread(gamma_ref, gamma)
            spread(cross_ref, cross)
            product(a_ref, vec, 1, 0, peer_ref)
            put_rows(peer_ref, gamma, cross)

        def later_piece(index, a_ref, vec, peer_ref):
            product(a_ref, vec, 1, index, peer_ref)

        def own_pieces(a_ref, vec, *refs):
            for index, ref in enumerate(refs):
                product(a_ref, vec, 0, index, ref)

        if in_two and by_block:
            return forward_in_two(wire, blocks)
        peer, gamma, cross, vec = call(
            first_piece,
            [pieces(wire)[0], scalar, scalar, ((feats, outs), BF16)],
            [states] + blocks,
        )
        got = [over_group(1, peer)]
        for index in range(1, levels):
            (peer,) = call(functools.partial(later_piece, index), [pieces(wire)[index]], [states, vec])
            got.append(over_group(1, peer))
        own = call(own_pieces, [((rows, outs), F32) for rows in piece_rows], [states, vec])
        return own, gamma, cross, got

    def forward_in_two(wire, blocks):
        early, late = [0, n_row - 1], list(range(1, n_row - 1))

        def product(a_ref, core_step, index, step, block_ref):
            start, rows = piece_starts[index], piece_rows[index]
            place = pl.ds(pl.multiple_of(token_place(core_step) + start, 64), rows)
            return jnp.dot(
                a_ref[place, pl.ds(row_place(step), feat_share)],
                body_of(block_ref),
                preferred_element_type=F32,
            )

        def summed(a_ref, core_step, index, steps, block_refs, total=None):
            for step, ref in zip(steps, block_refs):
                part = product(a_ref, core_step, index, step, ref)
                total = part if total is None else total + part
            return total

        def early_part(a_ref, *refs):
            ins, parts = refs[: len(early)], refs[len(early) :]
            for core_step in (1, 0):
                for index in range(levels):
                    parts[(1 - core_step) * levels + index][...] = summed(a_ref, core_step, index, early, ins)

        def first_piece(a_ref, part_ref, *refs):
            ins, (peer_ref, gamma_ref, cross_ref) = refs[:n_row], refs[n_row:]
            gamma = tree_sum([get_row(ref, 0) for ref in ins])
            cross = tree_sum([get_row(ref, 1) for ref in ins])
            spread(gamma_ref, gamma)
            spread(cross_ref, cross)
            total = summed(a_ref, 1, 0, late, [ins[step] for step in late], part_ref[...])
            peer_ref[pl.ds(0, piece_rows[0]), :] = total.astype(wire)
            put_rows(peer_ref, gamma, cross)

        def later_piece(index, a_ref, part_ref, *refs):
            *block_refs, peer_ref = refs
            peer_ref[...] = summed(a_ref, 1, index, late, block_refs, part_ref[...]).astype(wire)

        def own_pieces(a_ref, *refs):
            block_refs, refs = refs[: len(late)], refs[len(late) :]
            for index in range(levels):
                refs[levels + index][...] = summed(a_ref, 0, index, late, block_refs, refs[index][...])

        own_shapes = [((rows, outs), F32) for rows in piece_rows]
        late_blocks = [blocks[step] for step in late]
        parts = call(early_part, own_shapes * 2, [states] + [blocks[step] for step in early])
        peer, gamma, cross = call(
            first_piece, [pieces(wire)[0], scalar, scalar], [states, parts[0]] + blocks
        )
        got = [over_group(1, peer)]
        for index in range(1, levels):
            (peer,) = call(
                functools.partial(later_piece, index), [pieces(wire)[index]], [states, parts[index], *late_blocks]
            )
            got.append(over_group(1, peer))
        own = call(own_pieces, own_shapes, [states, *late_blocks] + list(parts[levels:]))
        return own, gamma, cross, got

    def pieces(wire):
        return [((rows + (0 if index else PAD), outs), wire) for index, rows in enumerate(piece_rows)]

    def swapped(step, sends):
        return [
            over_group(2 << ((index + step) % levels), send) for index, send in enumerate(sends)
        ]

    def join_cores(wire, own, gamma, cross, got):
        def kernel(own_ref, got_ref, *refs):
            *scalars, out_ref = refs
            place = pl.ds(0, own_ref.shape[0])
            out_ref[place, :] = (own_ref[...] + got_ref[place, :].astype(F32)).astype(wire)
            if scalars:
                put_rows(out_ref, *[ref[0:1, :] + get_row(got_ref, k) for k, ref in enumerate(scalars)])

        return [
            call(kernel, [shape], [own[index], got[index]] + ([] if index else [gamma, cross]))[0]
            for index, shape in enumerate(pieces(wire))
        ]

    def join_chips(wire, sent, got):
        def kernel(has_scalars, rows, own_ref, got_ref, out_ref):
            place = pl.ds(0, rows)
            both = own_ref[place, :].astype(F32) + got_ref[place, :].astype(F32)
            out_ref[place, :] = both.astype(wire)
            if has_scalars:
                put_rows(out_ref, *[get_row(own_ref, k) + get_row(got_ref, k) for k in range(2)])

        return [
            call(functools.partial(kernel, index == 0, piece_rows[index]), [shape], [sent[index], got[index]])[0]
            for index, shape in enumerate(pieces(wire))
        ]

    def image_of(last, sent, got, grad, before):
        def first_piece(own_ref, got_ref, grad_ref, *refs):
            old, (gamma_out, beta_out, sq_out, dir_out, *outputs) = refs[:-6 - more], refs[-6 - more :]
            gamma, cross = [get_row(own_ref, k) + get_row(got_ref, k) for k in range(2)]
            spread(gamma_out, gamma)
            direction = grad_ref[...]
            dir_sq = gamma
            beta = None
            if before:
                old_gamma, old_sq, old_dir = old[:3]
                beta = gamma / old_gamma[0:1, :]
                direction = direction + beta * old_dir[...]
                dir_sq = gamma + beta * (2.0 * cross + beta * old_sq[0:1, :])
                spread(beta_out, beta)
            else:
                spread(beta_out, gamma)
            dir_out[...] = direction
            spread(sq_out, dir_sq)
            part = piece_image(0, own_ref, got_ref, beta, old[3:], outputs)
            spread(outputs[-1], part)

        def later_piece(index, own_ref, got_ref, part_ref, beta_ref, *refs):
            count = len(shapes(index))
            old, outputs = refs[:-count], refs[-count:]
            part = part_ref[0:1, :] + piece_image(index, own_ref, got_ref, beta_ref[0:1, :], old, outputs)
            if not last and index + 1 == levels:
                put_rows(outputs[1], part)
            else:
                spread(outputs[-1], part)

        def piece_image(index, own_ref, got_ref, beta, old, outputs):
            place = pl.ds(0, piece_rows[index])
            image = own_ref[place, :].astype(F32) + got_ref[place, :].astype(F32)
            if before:
                image = image + beta * old[0][...]
            outputs[0][...] = image
            if not last:
                outputs[1][place, :] = image.astype(BF16)
            return column_sum(image * image)

        more = 0 if last else 1

        def shapes(index):
            rows = piece_rows[index]
            tail = PAD if index + 1 == levels else 0
            shape = [((rows, outs), F32)] + [((rows + tail, outs), BF16)] * more
            return shape + [scalar] if last or index + 1 < levels else shape

        gamma, beta, dir_sq, direction, image, *msg, part = call(
            first_piece,
            [scalar, scalar, scalar, feature_rows] + shapes(0),
            [sent[0], got[0], grad] + list(before[:3]) + list(before[3][:1] if before else ()),
        )
        images, msgs = [image], msg
        for index in range(1, levels):
            image, *msg = call(
                functools.partial(later_piece, index),
                shapes(index),
                [sent[index], got[index], part, beta] + list(before[3][index : index + 1] if before else ()),
            )
            if last or index + 1 < levels:
                *msg, part = msg
            images.append(image)
            msgs += msg
        return gamma, dir_sq, direction, images, msgs, part

    weights = ()
    residual, own, got = backward_first(ROW_WIRE[0])
    grad, msg = begin(own, got)
    before = ()
    for step in range(ITERS):
        own, gamma, cross, got = forward(CORE_WIRE[step], step in TWO_PARTS, msg)
        sent = join_cores(CHIP_WIRE[step][0], own, gamma, cross, got)
        got = swapped(0, sent)
        for level in range(1, levels):
            sent = join_chips(CHIP_WIRE[step][1], sent, got)
            got = swapped(level, sent)
        last = step + 1 == ITERS
        gamma, dir_sq, direction, images, msgs, part = image_of(last, sent, got, grad, before)
        if not last:
            own, delta, got = backward(
                ROW_WIRE[step + 1], msgs, [over_group(1, msg) for msg in msgs]
            )
            new, residual, grad, msg = advance(
                ROW_WIRE[step + 1], own, delta, got, gamma, dir_sq, grad, direction, images, weights, residual
            )
            weights = (new,)
            before = (gamma, dir_sq, direction, images)

    def both_cores(own_ref, got_ref, *refs):
        out_ref = refs[levels - 1]
        out_ref[...] = own_ref[...] + got_ref[...]

    vmem, anywhere = pl.BlockSpec(memory_space=pltpu.VMEM), pl.BlockSpec(memory_space=pl.ANY)
    delta, *later = pl.pallas_call(
        both_cores,
        out_shape=[jax.ShapeDtypeStruct(*scalar)] + [jax.ShapeDtypeStruct((rows, outs), F32) for rows in piece_rows[1:]],
        in_specs=[vmem, vmem] + [anywhere] * (levels - 1),
        out_specs=[vmem] + [anywhere] * (levels - 1),
        input_output_aliases={2 + index: 1 + index for index in range(levels - 1)},
        compiler_params=pltpu.CompilerParams(vmem_limit_bytes=LIMIT),
    )(part, over_group(1, part), *images[1:])
    images = [images[0], *later]
    other_images = [over_group(1, image) for image in images]
    other_residual = over_group(1, residual)
    got = {step: over_row(step, delta) for step in row_steps}
    deltas = [delta] + [got[step] for step in range(1, n_row)]

    def finish(*refs):
        delta_refs, refs = refs[:n_row], refs[n_row:]
        image_refs, refs = refs[:levels], refs[levels:]
        other_image_refs, refs = refs[:levels], refs[levels:]
        gamma_ref, sq_ref, ridge_ref, r_ref, other_r_ref, dir_ref, w_ref, w_out, r_out = refs
        image_sq = tree_sum([ref[0:1, :] for ref in delta_refs])
        alpha = gamma_ref[0:1, :] / (image_sq + ridge_ref[...] * sq_ref[0:1, :])
        w_out[...] = w_ref[...] + alpha * dir_ref[...]
        for core_step, old_ref, refs in ((0, r_ref, image_refs), (1, other_r_ref, other_image_refs)):
            for ref, start, rows in zip(refs, piece_starts, piece_rows):
                place = pl.ds(pl.multiple_of(token_place(core_step) + start, 64), rows)
                r_out[place, :] = old_ref[pl.ds(start, rows), :] - alpha * ref[...]

    weights, residual = call(
        finish,
        [feature_rows, ((tokens, outs), F32)],
        [*deltas, *images, *other_images, gamma, dir_sq, ridge, residual, other_residual, direction, *weights],
    )
    return weights, residual


def solution(mesh):
    placed = (P("row", "group"), P("row", None), P())
    return jax.shard_map(
        shards,
        mesh=mesh,
        in_specs=placed,
        out_specs=(P(("group", "row"), None), P("row", None)),
        check_vma=False,
    )
```

```python
import functools

import jax
import jax.numpy as jnp
from jax import lax
from jax.experimental import pallas as pl
from jax.experimental.pallas import tpu as pltpu
from jax.sharding import PartitionSpec as P

ITERS = 3
PAD = 16
TWO_PARTS = (1,)
F32 = jnp.float32
BF16 = jnp.bfloat16
F16 = jnp.float16
ROW_WIRE = (F16, F16, BF16)
CORE_WIRE = (F32, F32, F32)
CHIP_WIRE = ((BF16, BF16), (BF16, BF16), (BF16, BF16))
FIRST_PIECE = 9
ROW_ORDER = 1
LIMIT = 24 * 1024 * 1024


def tree_sum(terms):
    terms = list(terms)
    while len(terms) > 1:
        terms = [terms[i] + terms[i + 1] for i in range(0, len(terms), 2)]
    return terms[0]


def put_rows(ref, *values):
    rows = ref.shape[0] - PAD
    parts = []
    for value in values:
        high = value.astype(BF16).astype(F32)
        middle = (value - high).astype(BF16).astype(F32)
        parts += [high, middle, value - high - middle]
    shape = (PAD, ref.shape[1])
    index = lax.broadcasted_iota(jnp.int32, shape, 0)
    block = jnp.zeros(shape, F32)
    for place, part in enumerate(parts):
        block = jnp.where(index == place, jnp.broadcast_to(part, shape), block)
    ref[pl.ds(rows, PAD), :] = block.astype(ref.dtype)


def get_row(ref, which=0):
    rows = ref.shape[0] - PAD
    tail = ref[pl.ds(rows, PAD), :].astype(F32)
    at = 3 * which
    return tail[at : at + 1] + tail[at + 1 : at + 2] + tail[at + 2 : at + 3]


def exponent_of(value):
    return jnp.clip(jnp.floor(jnp.log2(jnp.maximum(value, 1e-36))), -119.0, 119.0)


def put_scaled(ref, exponent, value):
    rows = ref.shape[0] - PAD
    own = exponent_of(value)
    scaled = value * jnp.exp2(-own)
    high = scaled.astype(BF16).astype(F32)
    middle = (scaled - high).astype(BF16).astype(F32)
    parts = [exponent, own, high, 256.0 * middle, 65536.0 * (scaled - high - middle)]
    shape = (PAD, ref.shape[1])
    index = lax.broadcasted_iota(jnp.int32, shape, 0)
    block = jnp.zeros(shape, F32)
    for place, part in enumerate(parts):
        block = jnp.where(index == place, jnp.broadcast_to(part, shape), block)
    ref[pl.ds(rows, PAD), :] = block


def get_scaled(ref):
    rows = ref.shape[0] - PAD
    tail = ref[pl.ds(rows, PAD), :]
    value = tail[2:3] + tail[3:4] * (1.0 / 256.0) + tail[4:5] * (1.0 / 65536.0)
    return jnp.exp2(tail[0:1]), value * jnp.exp2(tail[1:2])


def body_of(ref):
    return ref[pl.ds(0, ref.shape[0] - PAD), :]


def column_sum(values):
    return jnp.sum(values, axis=0, keepdims=True)


def spread(ref, value):
    ref[...] = jnp.broadcast_to(value, ref.shape)


def call(kernel, outs, operands, scratch=()):
    vmem = pl.BlockSpec(memory_space=pltpu.VMEM)
    return pl.pallas_call(
        kernel,
        out_shape=[jax.ShapeDtypeStruct(shape, dtype) for shape, dtype in outs],
        in_specs=[vmem] * len(operands),
        out_specs=[vmem] * len(outs),
        scratch_shapes=scratch,
        compiler_params=pltpu.CompilerParams(vmem_limit_bytes=LIMIT),
    )(*operands)


def shards(states, targets, ridge):
    n_row = lax.axis_size("row")
    n_group = lax.axis_size("group")
    levels = (n_group // 2).bit_length() - 1
    tokens, feats = states.shape
    outs = targets.shape[1]
    feat_share = feats // n_row
    half = tokens // 2
    piece_rows = [half // levels] * levels
    if levels == 2:
        piece_rows = [half * FIRST_PIECE // 16, half - half * FIRST_PIECE // 16]
    piece_starts = [sum(piece_rows[:index]) for index in range(levels)]
    row_steps = list(range(1, n_row))[::ROW_ORDER]
    block = 256
    ridge = ridge.reshape(1, outs)
    scalar = ((8, outs), F32)
    feature_rows = ((feat_share, outs), F32)
    token_rows = ((half, outs), F32)

    def over_row(step, value):
        return lax.ppermute(value, "row", [(i, i ^ step) for i in range(n_row)])

    def over_group(step, value):
        return lax.ppermute(value, "group", [(i, i ^ step) for i in range(n_group)])

    def row_place(step):
        return pl.multiple_of((lax.axis_index("row") ^ step) * feat_share, feat_share)

    def token_place(core_step):
        core = (lax.axis_index("group") % 2) ^ core_step
        return pl.multiple_of(core * half, half)

    def cut(wire, prod, delta, own_ref, msg_refs):
        own_ref[...] = prod[pl.ds(row_place(0), feat_share), :]
        if wire == F16:
            exponent = exponent_of(jnp.max(jnp.abs(prod[...]), axis=0, keepdims=True))
            factor = jnp.exp2(-exponent)
        for step, ref in zip(row_steps, msg_refs):
            part = prod[pl.ds(row_place(step), feat_share), :]
            if wire == F16:
                ref[pl.ds(0, feat_share), :] = part * factor
                put_scaled(ref, exponent, delta)
            else:
                ref[pl.ds(0, feat_share), :] = part.astype(wire)
                put_rows(ref, delta)

    def put_block(wire, ref, part, delta):
        if wire == F16:
            exponent = exponent_of(jnp.max(jnp.abs(part), axis=0, keepdims=True))
            ref[pl.ds(0, feat_share), :] = part * jnp.exp2(-exponent)
            put_scaled(ref, exponent, delta)
        else:
            ref[pl.ds(0, feat_share), :] = part.astype(wire)
            put_rows(ref, delta)

    by_block = feat_share % 128 == 0

    def columns(step):
        return pl.ds(row_place(step), feat_share)

    def cut_shapes(wire):
        return [((feat_share + PAD, outs), F32 if wire == F16 else wire)] * (n_row - 1)

    def scattered(wire, sends):
        got = {step: over_row(step, send.astype(wire)) for step, send in zip(row_steps, sends)}
        got = [got[step] for step in range(1, n_row)]
        return [send.astype(F32) if wire == F16 else send for send in got]

    def backward_first(wire):
        def split(t_ref, turned_ref, r_out):
            for start in range(0, tokens, block):
                whole = t_ref[start : start + block, :]
                high = whole.astype(BF16)
                turned_ref[0:outs, start : start + block] = high.T
                turned_ref[outs : 2 * outs, start : start + block] = (whole - high.astype(F32)).astype(BF16).T
            r_out[...] = t_ref[pl.ds(token_place(0), half), :]

        def product(a_ref, turned_ref, own_ref, *refs):
            *msg_refs, prod = refs
            for start in range(0, feats, block):
                cols = slice(start, start + block)
                part = jnp.dot(turned_ref[...], a_ref[:, cols], preferred_element_type=F32)
                prod[cols, :] = (part[0:outs] + part[outs : 2 * outs]).T
            cut(wire, prod, jnp.zeros((1, outs), F32), own_ref, msg_refs)

        def block_product(a_ref, turned_ref, step):
            part = jnp.dot(turned_ref[...], a_ref[:, columns(step)], preferred_element_type=F32)
            return (part[0:outs] + part[outs : 2 * outs]).T

        def messages(a_ref, turned_ref, *msg_refs):
            for step, ref in zip(row_steps, msg_refs):
                put_block(wire, ref, block_product(a_ref, turned_ref, step), jnp.zeros((1, outs), F32))

        def own_block(a_ref, turned_ref, own_ref):
            own_ref[...] = block_product(a_ref, turned_ref, 0)

        turned, residual = call(split, [((2 * outs, tokens), BF16), token_rows], [targets])
        if by_block:
            got = scattered(wire, call(messages, cut_shapes(wire), [states, turned]))
            (own,) = call(own_block, [feature_rows], [states, turned])
            return residual, own, got
        own, *sends = call(
            product,
            [feature_rows] + cut_shapes(wire),
            [states, turned],
            [pltpu.VMEM((feats, outs), F32)],
        )
        return residual, own, scattered(wire, sends)

    def backward(wire, mine, theirs):
        def half_product(a_ref, refs, core_step, cols):
            total = None
            for ref, start, rows in zip(refs, piece_starts, piece_rows):
                place = pl.ds(pl.multiple_of(token_place(core_step) + start, 64), rows)
                part = jnp.dot(ref[pl.ds(0, rows), :].T, a_ref[place, cols], preferred_element_type=F32)
                total = part if total is None else total + part
            return total

        def first_half(a_ref, *refs):
            *mine_refs, part_ref = refs
            for start in range(0, feats, block):
                cols = slice(start, start + block)
                part_ref[:, cols] = half_product(a_ref, mine_refs, 0, cols)

        def second_half(a_ref, *refs):
            mine_ref, theirs_refs = refs[0], refs[1 : levels + 1]
            part_ref, own_ref, delta_ref, *msg_refs, prod = refs[levels + 1 :]
            delta = get_row(mine_ref) + get_row(theirs_refs[-1])
            spread(delta_ref, delta)
            for start in range(0, feats, block):
                cols = slice(start, start + block)
                prod[cols, :] = (part_ref[:, cols] + half_product(a_ref, theirs_refs, 1, cols)).T
            cut(wire, prod, delta, own_ref, msg_refs)

        def block_product(a_ref, part_ref, refs, step):
            return (part_ref[:, columns(step)] + half_product(a_ref, refs, 1, columns(step))).T

        def messages(a_ref, *refs):
            mine_ref, theirs_refs, part_ref = refs[0], refs[1 : levels + 1], refs[levels + 1]
            delta_ref, *msg_refs = refs[levels + 2 :]
            delta = get_row(mine_ref) + get_row(theirs_refs[-1])
            spread(delta_ref, delta)
            for step, ref in zip(row_steps, msg_refs):
                put_block(wire, ref, block_product(a_ref, part_ref, theirs_refs, step), delta)

        def own_block(a_ref, *refs):
            *theirs_refs, part_ref, own_ref = refs
            own_ref[...] = block_product(a_ref, part_ref, theirs_refs, 0)

        (part,) = call(first_half, [((outs, feats), F32)], [states, *mine])
        if by_block:
            delta, *sends = call(
                messages, [scalar] + cut_shapes(wire), [states, mine[-1], *theirs, part]
            )
            got = scattered(wire, sends)
            (own,) = call(own_block, [feature_rows], [states, *theirs, part])
            return own, delta, got
        own, delta, *sends = call(
            second_half,
            [feature_rows, scalar] + cut_shapes(wire),
            [states, mine[-1], *theirs, part],
            [pltpu.VMEM((feats, outs), F32)],
        )
        return own, delta, scattered(wire, sends)

    def begin(own, got):
        def kernel(own_ref, *refs):
            ins, (grad_ref, msg_ref) = refs[: n_row - 1], refs[n_row - 1 :]
            grad = own_ref[...]
            for ref in ins:
                grad = grad + get_scaled(ref)[0] * body_of(ref)
            grad_ref[...] = grad
            msg_ref[pl.ds(0, feat_share), :] = grad.astype(BF16)
            put_rows(msg_ref, column_sum(grad * grad), jnp.zeros((1, outs), F32))

        return call(kernel, [feature_rows, ((feat_share + PAD, outs), BF16)], [own] + got)

    def advance(wire, own, delta, got, gamma, dir_sq, grad, direction, images, weights, residual):
        def critical(own_ref, delta_ref, *refs):
            ins = refs[: n_row - 1]
            gamma_ref, sq_ref, grad_ref, dir_ref, ridge_ref, grad_out, msg_ref, alpha_ref = refs[n_row - 1 :]
            if wire == F16:
                tails = [get_scaled(ref) for ref in ins]
            else:
                tails = [(1.0, get_row(ref)) for ref in ins]
            image_sq = tree_sum([delta_ref[0:1, :]] + [value for _, value in tails])
            alpha = gamma_ref[0:1, :] / (image_sq + ridge_ref[...] * sq_ref[0:1, :])
            spread(alpha_ref, alpha)
            prod = own_ref[...]
            for ref, (scale, _) in zip(ins, tails):
                prod = prod + scale * body_of(ref).astype(F32)
            old_dir = dir_ref[...]
            new = grad_ref[...] - alpha * (prod + ridge_ref[...] * old_dir)
            msg_ref[pl.ds(0, feat_share), :] = new.astype(BF16)
            put_rows(msg_ref, column_sum(new * new), column_sum(new * old_dir))
            grad_out[...] = new

        def updates(alpha_ref, dir_ref, r_ref, *refs):
            image_refs = refs[:levels]
            *w_ref, w_out, r_out = refs[levels:]
            alpha = alpha_ref[0:1, :]
            step_taken = alpha * dir_ref[...]
            w_out[...] = w_ref[0][...] + step_taken if w_ref else step_taken
            for ref, start, rows in zip(image_refs, piece_starts, piece_rows):
                place = pl.ds(start, rows)
                r_out[place, :] = r_ref[place, :] - alpha * ref[...]

        grad, msg, alpha = call(
            critical,
            [feature_rows, ((feat_share + PAD, outs), BF16), scalar],
            [own, delta, *got, gamma, dir_sq, grad, direction, ridge],
        )
        new_weights, new_residual = call(
            updates, [feature_rows, token_rows], [alpha, direction, residual, *images, *weights]
        )
        return new_weights, new_residual, grad, msg

    def forward(wire, in_two, msg):
        got = {step: over_row(step, msg) for step in row_steps}
        blocks = [msg] + [got[step] for step in range(1, n_row)]

        def product(a_ref, vec, core_step, index, ref):
            start, rows = piece_starts[index], piece_rows[index]
            place = pl.ds(pl.multiple_of(token_place(core_step) + start, 64), rows)
            part = jnp.dot(a_ref[place, :], vec[...], preferred_element_type=F32)
            ref[pl.ds(0, rows), :] = part.astype(ref.dtype)

        def first_piece(a_ref, *refs):
            ins = refs[:n_row]
            peer_ref, gamma_ref, cross_ref, vec = refs[n_row:]
            for step, ref in enumerate(ins):
                vec[pl.ds(row_place(step), feat_share), :] = body_of(ref)
            gamma = tree_sum([get_row(ref, 0) for ref in ins])
            cross = tree_sum([get_row(ref, 1) for ref in ins])
            spread(gamma_ref, gamma)
            spread(cross_ref, cross)
            product(a_ref, vec, 1, 0, peer_ref)
            put_rows(peer_ref, gamma, cross)

        def later_piece(index, a_ref, vec, peer_ref):
            product(a_ref, vec, 1, index, peer_ref)

        def own_pieces(a_ref, vec, *refs):
            for index, ref in enumerate(refs):
                product(a_ref, vec, 0, index, ref)

        if in_two and by_block:
            return forward_in_two(wire, blocks)
        peer, gamma, cross, vec = call(
            first_piece,
            [pieces(wire)[0], scalar, scalar, ((feats, outs), BF16)],
            [states] + blocks,
        )
        got = [over_group(1, peer)]
        for index in range(1, levels):
            (peer,) = call(functools.partial(later_piece, index), [pieces(wire)[index]], [states, vec])
            got.append(over_group(1, peer))
        own = call(own_pieces, [((rows, outs), F32) for rows in piece_rows], [states, vec])
        return own, gamma, cross, got

    def forward_in_two(wire, blocks):
        early, late = [0, n_row - 1], list(range(1, n_row - 1))

        def product(a_ref, core_step, index, step, block_ref):
            start, rows = piece_starts[index], piece_rows[index]
            place = pl.ds(pl.multiple_of(token_place(core_step) + start, 64), rows)
            return jnp.dot(
                a_ref[place, pl.ds(row_place(step), feat_share)],
                body_of(block_ref),
                preferred_element_type=F32,
            )

        def summed(a_ref, core_step, index, steps, block_refs, total=None):
            for step, ref in zip(steps, block_refs):
                part = product(a_ref, core_step, index, step, ref)
                total = part if total is None else total + part
            return total

        def early_part(a_ref, *refs):
            ins, parts = refs[: len(early)], refs[len(early) :]
            for core_step in (1, 0):
                for index in range(levels):
                    parts[(1 - core_step) * levels + index][...] = summed(a_ref, core_step, index, early, ins)

        def first_piece(a_ref, part_ref, *refs):
            ins, (peer_ref, gamma_ref, cross_ref) = refs[:n_row], refs[n_row:]
            gamma = tree_sum([get_row(ref, 0) for ref in ins])
            cross = tree_sum([get_row(ref, 1) for ref in ins])
            spread(gamma_ref, gamma)
            spread(cross_ref, cross)
            total = summed(a_ref, 1, 0, late, [ins[step] for step in late], part_ref[...])
            peer_ref[pl.ds(0, piece_rows[0]), :] = total.astype(wire)
            put_rows(peer_ref, gamma, cross)

        def later_piece(index, a_ref, part_ref, *refs):
            *block_refs, peer_ref = refs
            peer_ref[...] = summed(a_ref, 1, index, late, block_refs, part_ref[...]).astype(wire)

        def own_pieces(a_ref, *refs):
            block_refs, refs = refs[: len(late)], refs[len(late) :]
            for index in range(levels):
                refs[levels + index][...] = summed(a_ref, 0, index, late, block_refs, refs[index][...])

        own_shapes = [((rows, outs), F32) for rows in piece_rows]
        late_blocks = [blocks[step] for step in late]
        parts = call(early_part, own_shapes * 2, [states] + [blocks[step] for step in early])
        peer, gamma, cross = call(
            first_piece, [pieces(wire)[0], scalar, scalar], [states, parts[0]] + blocks
        )
        got = [over_group(1, peer)]
        for index in range(1, levels):
            (peer,) = call(
                functools.partial(later_piece, index), [pieces(wire)[index]], [states, parts[index], *late_blocks]
            )
            got.append(over_group(1, peer))
        own = call(own_pieces, own_shapes, [states, *late_blocks] + list(parts[levels:]))
        return own, gamma, cross, got

    def pieces(wire):
        return [((rows + (0 if index else PAD), outs), wire) for index, rows in enumerate(piece_rows)]

    def swapped(step, sends):
        return [
            over_group(2 << ((index + step) % levels), send) for index, send in enumerate(sends)
        ]

    def join_cores(wire, own, gamma, cross, got):
        def kernel(own_ref, got_ref, *refs):
            *scalars, out_ref = refs
            place = pl.ds(0, own_ref.shape[0])
            out_ref[place, :] = (own_ref[...] + got_ref[place, :].astype(F32)).astype(wire)
            if scalars:
                put_rows(out_ref, *[ref[0:1, :] + get_row(got_ref, k) for k, ref in enumerate(scalars)])

        return [
            call(kernel, [shape], [own[index], got[index]] + ([] if index else [gamma, cross]))[0]
            for index, shape in enumerate(pieces(wire))
        ]

    def join_chips(wire, sent, got):
        def kernel(has_scalars, rows, own_ref, got_ref, out_ref):
            place = pl.ds(0, rows)
            both = own_ref[place, :].astype(F32) + got_ref[place, :].astype(F32)
            out_ref[place, :] = both.astype(wire)
            if has_scalars:
                put_rows(out_ref, *[get_row(own_ref, k) + get_row(got_ref, k) for k in range(2)])

        return [
            call(functools.partial(kernel, index == 0, piece_rows[index]), [shape], [sent[index], got[index]])[0]
            for index, shape in enumerate(pieces(wire))
        ]

    def image_of(last, sent, got, grad, before):
        def first_piece(own_ref, got_ref, grad_ref, *refs):
            old, (gamma_out, beta_out, sq_out, dir_out, *outputs) = refs[:-6 - more], refs[-6 - more :]
            gamma, cross = [get_row(own_ref, k) + get_row(got_ref, k) for k in range(2)]
            spread(gamma_out, gamma)
            direction = grad_ref[...]
            dir_sq = gamma
            beta = None
            if before:
                old_gamma, old_sq, old_dir = old[:3]
                beta = gamma / old_gamma[0:1, :]
                direction = direction + beta * old_dir[...]
                dir_sq = gamma + beta * (2.0 * cross + beta * old_sq[0:1, :])
                spread(beta_out, beta)
            else:
                spread(beta_out, gamma)
            dir_out[...] = direction
            spread(sq_out, dir_sq)
            part = piece_image(0, own_ref, got_ref, beta, old[3:], outputs)
            spread(outputs[-1], part)

        def later_piece(index, own_ref, got_ref, part_ref, beta_ref, *refs):
            count = len(shapes(index))
            old, outputs = refs[:-count], refs[-count:]
            part = part_ref[0:1, :] + piece_image(index, own_ref, got_ref, beta_ref[0:1, :], old, outputs)
            if not last and index + 1 == levels:
                put_rows(outputs[1], part)
            else:
                spread(outputs[-1], part)

        def piece_image(index, own_ref, got_ref, beta, old, outputs):
            place = pl.ds(0, piece_rows[index])
            image = own_ref[place, :].astype(F32) + got_ref[place, :].astype(F32)
            if before:
                image = image + beta * old[0][...]
            outputs[0][...] = image
            if not last:
                outputs[1][place, :] = image.astype(BF16)
            return column_sum(image * image)

        more = 0 if last else 1

        def shapes(index):
            rows = piece_rows[index]
            tail = PAD if index + 1 == levels else 0
            shape = [((rows, outs), F32)] + [((rows + tail, outs), BF16)] * more
            return shape + [scalar] if last or index + 1 < levels else shape

        gamma, beta, dir_sq, direction, image, *msg, part = call(
            first_piece,
            [scalar, scalar, scalar, feature_rows] + shapes(0),
            [sent[0], got[0], grad] + list(before[:3]) + list(before[3][:1] if before else ()),
        )
        images, msgs = [image], msg
        for index in range(1, levels):
            image, *msg = call(
                functools.partial(later_piece, index),
                shapes(index),
                [sent[index], got[index], part, beta] + list(before[3][index : index + 1] if before else ()),
            )
            if last or index + 1 < levels:
                *msg, part = msg
            images.append(image)
            msgs += msg
        return gamma, dir_sq, direction, images, msgs, part

    weights = ()
    residual, own, got = backward_first(ROW_WIRE[0])
    grad, msg = begin(own, got)
    before = ()
    for step in range(ITERS):
        own, gamma, cross, got = forward(CORE_WIRE[step], step in TWO_PARTS, msg)
        sent = join_cores(CHIP_WIRE[step][0], own, gamma, cross, got)
        got = swapped(0, sent)
        for level in range(1, levels):
            sent = join_chips(CHIP_WIRE[step][1], sent, got)
            got = swapped(level, sent)
        last = step + 1 == ITERS
        gamma, dir_sq, direction, images, msgs, part = image_of(last, sent, got, grad, before)
        if not last:
            own, delta, got = backward(
                ROW_WIRE[step + 1], msgs, [over_group(1, msg) for msg in msgs]
            )
            new, residual, grad, msg = advance(
                ROW_WIRE[step + 1], own, delta, got, gamma, dir_sq, grad, direction, images, weights, residual
            )
            weights = (new,)
            before = (gamma, dir_sq, direction, images)

    def both_cores(own_ref, got_ref, *refs):
        out_ref = refs[levels - 1]
        out_ref[...] = own_ref[...] + got_ref[...]

    vmem, anywhere = pl.BlockSpec(memory_space=pltpu.VMEM), pl.BlockSpec(memory_space=pl.ANY)
    delta, *later = pl.pallas_call(
        both_cores,
        out_shape=[jax.ShapeDtypeStruct(*scalar)] + [jax.ShapeDtypeStruct((rows, outs), F32) for rows in piece_rows[1:]],
        in_specs=[vmem, vmem] + [anywhere] * (levels - 1),
        out_specs=[vmem] + [anywhere] * (levels - 1),
        input_output_aliases={2 + index: 1 + index for index in range(levels - 1)},
        compiler_params=pltpu.CompilerParams(vmem_limit_bytes=LIMIT),
    )(part, over_group(1, part), *images[1:])
    images = [images[0], *later]
    other_images = [over_group(1, image) for image in images]
    other_residual = over_group(1, residual)
    got = {step: over_row(step, delta) for step in row_steps}
    deltas = [delta] + [got[step] for step in range(1, n_row)]

    def finish(*refs):
        delta_refs, refs = refs[:n_row], refs[n_row:]
        image_refs, refs = refs[:levels], refs[levels:]
        other_image_refs, refs = refs[:levels], refs[levels:]
        gamma_ref, sq_ref, ridge_ref, r_ref, other_r_ref, dir_ref, w_ref, w_out, r_out = refs
        image_sq = tree_sum([ref[0:1, :] for ref in delta_refs])
        alpha = gamma_ref[0:1, :] / (image_sq + ridge_ref[...] * sq_ref[0:1, :])
        w_out[...] = w_ref[...] + alpha * dir_ref[...]
        for core_step, old_ref, refs in ((0, r_ref, image_refs), (1, other_r_ref, other_image_refs)):
            for ref, start, rows in zip(refs, piece_starts, piece_rows):
                place = pl.ds(pl.multiple_of(token_place(core_step) + start, 64), rows)
                r_out[place, :] = old_ref[pl.ds(start, rows), :] - alpha * ref[...]

    weights, residual = call(
        finish,
        [feature_rows, ((tokens, outs), F32)],
        [*deltas, *images, *other_images, gamma, dir_sq, ridge, residual, other_residual, direction, *weights],
    )
    return weights, residual


def solution(mesh):
    placed = (P("row", "group"), P("row", None), P())
    return jax.shard_map(
        shards,
        mesh=mesh,
        in_specs=placed,
        out_specs=(P(("group", "row"), None), P("row", None)),
        check_vma=False,
    )
```
